32 devices in a mesh: seg: 8 (over z, x), head: 4 (over y, core).
Axes of the slice: x: 2, y: 2, z: 4, core: 2. Of those that a mesh axis runs over, the one named last changes fastest.
Arguments:
- queries: bfloat16 [2048, 1536], P(('seg', 'head')), may hold values from -8 to 8
- key_rows: bfloat16 [2048, 1536], P(('seg', 'head')), may hold values from -8 to 8
- value_rows: bfloat16 [2048, 1536], P(('seg', 'head')), may hold values from -6 to 6
- w_first: float32 [24, 64, 256], P('head'), may hold values from -0.75 to 0.75
- w_second: float32 [24, 256, 64], P('head'), may hold values from -0.375 to 0.375
- gate_pairs: float32 [2, 1536], P(None, 'head'), may hold values from 0.3 to 1.5
Outputs:
- mixed: float32 [2048, 1536], P('seg', 'head')
The draws below stay inside these ranges and needn't reach their ends.
All inputs are finite; a program needn't handle non-finite values.
Results may differ from the reference program's by a relative error of at most 0.0011.
Values may be sent and summed in bfloat16 or wider, within the bound.
No kernel may reach another device: no remote copies, remote signals or barrier semaphores. Data moves between devices by JAX's collectives and lax.ppermute only.
A program may use at most 128 MiB of HBM per device.

```python
import jax
import jax.numpy as jnp
from jax import lax

HEADS = 24
HEAD_DIM = 64
INNER = 256
SEG = 2048
PART = 256
TOKENS = 2048


def drawn_pair(key):
    row_count = TOKENS
    col_count = HEADS * HEAD_DIM
    base_query = jax.random.truncated_normal(jax.random.fold_in(key, 11), -4.0, 4.0, (row_count, col_count), jnp.float32)
    base_key = jax.random.truncated_normal(jax.random.fold_in(key, 12), -4.0, 4.0, (row_count, col_count), jnp.float32)
    return (base_query, base_key)


def draw_queries(key, part):
    return drawn_pair(key)[0].astype(jnp.bfloat16)


def draw_key_rows(key, part):
    return drawn_pair(key)[1].astype(jnp.bfloat16)


def block_levels(stream_key, extent, pieces, low, largest):
    def one(position, parts):
        heights = jax.random.uniform(jax.random.fold_in(jax.random.fold_in(stream_key, 6), position), (parts,), jnp.float32, low / len(pieces), largest / len(pieces))
        return jnp.repeat(jnp.exp(heights), extent[position] // parts).reshape((-1,) + (1,) * (len(extent) - position - 1))

    gain = one(*pieces[0])
    for cut in pieces[1:]:
        gain = gain * one(*cut)
    return gain


def bell_draw(stream_key, dims, deviation, bound, pieces=(), held_as=jnp.bfloat16):
    drawn = jax.random.normal(stream_key, dims, jnp.float32) * deviation
    if len(pieces) > 0:
        drawn = block_levels(stream_key, dims, pieces, -0.22, 0.18) * drawn
    return jnp.clip(drawn, min=-bound, max=bound).astype(held_as)


def setup_inputs(seed: int = 0) -> dict:
    seeds = jax.random.split(jax.random.key(seed), 7)
    queries = draw_queries(jax.random.fold_in(seeds[6], 71), 0)
    key_rows = draw_key_rows(jax.random.fold_in(seeds[6], 71), 0)
    value_rows = bell_draw(seeds[2], (TOKENS, HEADS * HEAD_DIM), 1.0, 6.0, ((0, 32),))
    w_first = bell_draw(seeds[3], (HEADS, HEAD_DIM, INNER), HEAD_DIM ** -0.5, 0.75, ((0, 4),), jnp.float32)
    w_second = bell_draw(seeds[4], (HEADS, INNER, HEAD_DIM), INNER ** -0.5, 0.375, ((0, 4),), jnp.float32)
    gate_pairs = jnp.clip(0.3 + 1.2 * jax.random.uniform(seeds[5], (2, HEADS * HEAD_DIM), jnp.float32) ** block_levels(seeds[5], (2, HEADS * HEAD_DIM), ((1, 4),), -0.2, 0.2), 0.3, 1.5)
    return dict(queries=queries, key_rows=key_rows, value_rows=value_rows, w_first=w_first, w_second=w_second, gate_pairs=gate_pairs)


inner_rate = 0.05
norm_epsilon = 1e-05
highest = lax.Precision.HIGHEST

def inner_model(inputs, first, second):
    hidden = jnp.einsum('nhd,hdf->nhf', inputs, first, precision=highest)
    mapped = jnp.einsum('nhf,hfd->nhd', jax.nn.gelu(hidden), second, precision=highest)
    centre = mapped - lax.optimization_barrier(jnp.mean(mapped, axis=-1, keepdims=True))
    spread = lax.optimization_barrier(jnp.mean(centre * centre, axis=-1, keepdims=True))
    return centre * lax.rsqrt(spread + norm_epsilon)

def inner_loss(first, second, inputs, target):
    error = inner_model(inputs, first, second) - target
    return 0.5 * jnp.sum(error * error) / inputs.shape[0]

def segment_attention(query_rows, key_block, value_block):
    head_count = query_rows.shape[1] // HEAD_DIM

    def head_step(head_index, result):
        start = head_index * HEAD_DIM
        head_query = lax.dynamic_slice_in_dim(query_rows, start, HEAD_DIM, 1)
        head_key = lax.dynamic_slice_in_dim(key_block, start, HEAD_DIM, 1)
        head_value = lax.dynamic_slice_in_dim(value_block, start, HEAD_DIM, 1)
        scores = lax.dot_general(head_query, head_key, (((1,), (1,)), ((), ())), preferred_element_type=jnp.float32) * HEAD_DIM ** (-0.5)
        scores = scores - lax.optimization_barrier(jnp.max(scores, axis=-1, keepdims=True))
        expon = jnp.exp(scores)
        weights = (expon / lax.optimization_barrier(jnp.sum(expon, axis=-1, keepdims=True))).astype(jnp.bfloat16)
        attended = jnp.dot(weights, head_value, preferred_element_type=jnp.float32)
        return lax.dynamic_update_slice_in_dim(result, attended, start, 1)
    return lax.fori_loop(0, head_count, head_step, jnp.zeros(query_rows.shape, jnp.float32))

def reference(queries, key_rows, value_rows, w_first, w_second, gate_pairs):
    token_count, width = queries.shape
    block_count = token_count // PART
    segment_count = token_count // SEG

    def one_segment(index):
        start = (index * SEG).astype(jnp.int32)
        return segment_attention(lax.dynamic_slice_in_dim(queries, start, SEG, 0), lax.dynamic_slice_in_dim(key_rows, start, SEG, 0), lax.dynamic_slice_in_dim(value_rows, start, SEG, 0))
    attention = lax.map(one_segment, jnp.arange(segment_count, dtype=jnp.int32)).reshape(token_count, width)

    def block_rows(array, index):
        start = (index * PART).astype(jnp.int32)
        return lax.dynamic_slice_in_dim(array, start, PART, 0).astype(jnp.float32).reshape(PART, HEADS, HEAD_DIM)

    def block_grad(index):
        inputs = block_rows(key_rows, index)
        target = block_rows(value_rows, index) - inputs
        return jax.grad(inner_loss, argnums=(0, 1))(w_first, w_second, inputs, target)
    grad_first, grad_second = lax.map(block_grad, jnp.arange(block_count, dtype=jnp.int32))
    ahead_first = jnp.cumsum(grad_first, axis=0)
    ahead_second = jnp.cumsum(grad_second, axis=0)
    behind_first = jnp.flip(jnp.cumsum(jnp.flip(grad_first, 0), axis=0), 0)
    behind_second = jnp.flip(jnp.cumsum(jnp.flip(grad_second, 0), axis=0), 0)
    gate_forward = jnp.tanh(gate_pairs[0])
    gate_backward = jnp.tanh(gate_pairs[1])

    def block_out(operands):
        index, af_first, af_second, bh_first, bh_second, attended = operands
        inputs = block_rows(queries, index)
        forward_out = inputs + inner_model(inputs, w_first - inner_rate * af_first, w_second - inner_rate * af_second)
        backward_out = inputs + inner_model(inputs, w_first - inner_rate * bh_first, w_second - inner_rate * bh_second)
        return attended + gate_forward * forward_out.reshape(PART, width) + gate_backward * backward_out.reshape(PART, width)
    mixed = lax.map(block_out, (jnp.arange(block_count, dtype=jnp.int32), ahead_first, ahead_second, behind_first, behind_second, attention.reshape(block_count, PART, width)))
    return mixed.reshape(token_count, width)
```

```python
import functools

import jax
import jax.numpy as jnp
from jax import lax
from jax.experimental import pallas as pl
from jax.experimental.pallas import tpu as pltpu
from jax.sharding import PartitionSpec as P

HEAD_DIM = 64
GROUP = 8
LANES = 2 * HEAD_DIM

inner_rate = 0.05
norm_epsilon = 1e-05
LOG2E = 1.4426950408889634
GELU_A = 0.7978845608028654
GELU_B = 0.044715

f32, bf16 = (jnp.float32, jnp.bfloat16)
NN = (((1,), (0,)), ((), ()))
NT = (((1,), (1,)), ((), ()))
TN = (((0,), (0,)), ((), ()))


def dot(a, b, dims):
    return lax.dot_general(a, b, dims, preferred_element_type=f32)


def split(x):
    high = x.astype(bf16)
    return high, (x - high.astype(f32)).astype(bf16)


def half_turn(x):
    return jnp.concatenate([x[:, HEAD_DIM:], x[:, :HEAD_DIM]], axis=1)


def left_half(rows):
    return lax.broadcasted_iota(jnp.int32, (rows, LANES), 1) < HEAD_DIM


def gelu(z):
    t = jnp.tanh(z * (GELU_A + (GELU_A * GELU_B) * (z * z)))
    half = 0.5 * z
    return half + half * t


def gelu_and_slope(z):
    z2 = z * z
    t = jnp.tanh(z * (GELU_A + (GELU_A * GELU_B) * z2))
    a = 0.5 + 0.5 * t
    return z * a, a + z * (2 * GELU_A + (6 * GELU_A * GELU_B) * z2) * (a * (1 - a))


def centred(second):
    return second - jnp.mean(second, axis=0, keepdims=True)


def project(hidden, second):
    high, low = hidden
    second_high, second_low = split(second)
    return dot(high, second_high, NT) + dot(high, second_low, NT) + dot(low, second_high, NT)


def norm_scale(u):
    return lax.rsqrt(jnp.mean(u * u, axis=1, keepdims=True) + norm_epsilon)


def pack_kernel(q_ref, k_ref, v_ref, kv_ref, qq_ref, *, heads_here, sides):
    rows, width = q_ref.shape
    left = left_half(rows)
    left_q = left_half(rows // 2)
    for pair in range(width // LANES):
        cols = slice(pair * LANES, (pair + 1) * LANES)
        k, v, q = (k_ref[:, cols], v_ref[:, cols], q_ref[:, cols])
        k_turned, v_turned = (half_turn(k), half_turn(v))
        qa, qb = (q[: rows // 2], q[rows // 2 :])
        qa_turned, qb_turned = (half_turn(qa), half_turn(qb))
        for odd in range(2):
            head = 2 * pair + odd
            place = (head % heads_here) * sides + head // heads_here
            if odd:
                kv_ref[place] = jnp.where(left, k_turned, v)
                qq_ref[place] = jnp.where(left_q, qa_turned, qb)
            else:
                kv_ref[place] = jnp.where(left, k, v_turned)
                qq_ref[place] = jnp.where(left_q, qa, qb_turned)
    for place in range(heads_here * sides, kv_ref.shape[0]):
        kv_ref[place] = jnp.zeros(kv_ref.shape[1:], bf16)
        qq_ref[place] = jnp.zeros(qq_ref.shape[1:], bf16)


def pack(queries, key_rows, value_rows, heads_here, sides):
    rows = queries.shape[0]
    places = GROUP * sides
    return pl.pallas_call(
        functools.partial(pack_kernel, heads_here=heads_here, sides=sides),
        out_shape=(
            jax.ShapeDtypeStruct((places, rows, LANES), bf16),
            jax.ShapeDtypeStruct((places, rows // 2, LANES), bf16),
        ),
        name="pack",
    )(queries, key_rows, value_rows)


def gradient_kernel(place_ref, kv_ref, first_ref, second_ref, sum_first_ref, sum_second_ref):
    batches, dim, inner = sum_first_ref.shape
    part = kv_ref.shape[0] // batches
    left = left_half(part)
    first = jnp.concatenate(split(first_ref[0]), axis=0)
    second = second_ref[0].T
    second_centred = centred(second)
    second_high, second_low = split(second)
    sum_first = jnp.zeros((dim, inner), f32)
    sum_second = jnp.zeros((dim, inner), f32)
    for b in range(batches):
        kv = kv_ref[b * part : (b + 1) * part, :]
        vk = half_turn(kv)
        k, v = (kv[:, :dim], vk[:, :dim])
        hidden, slope = gelu_and_slope(dot(jnp.where(left, kv, vk), first, NN))
        h_high, h_low = split(hidden)
        u = project((h_high, h_low), second_centred)
        r = norm_scale(u)
        n = u * r
        error = n - v.astype(f32) + k.astype(f32)
        du = (r * (1.0 / part)) * (
            error
            - jnp.mean(error, axis=1, keepdims=True)
            - n * jnp.mean(error * n, axis=1, keepdims=True)
        )
        du_high, du_low = split(du)
        sum_second = sum_second + (
            dot(du_high, h_high, TN) + dot(du_high, h_low, TN) + dot(du_low, h_high, TN)
        )
        dh = dot(du_high, second_high, NN) + dot(du_low, second_high, NN) + dot(du_high, second_low, NN)
        dz_high, dz_low = split(dh * slope)
        sum_first = sum_first + (dot(k, dz_high, TN) + dot(k, dz_low, TN))
        sum_first_ref[b] = sum_first
        sum_second_ref[b] = sum_second


def whole(shape):
    return pl.BlockSpec(shape, lambda i, place: (0,) * len(shape))


def chosen(shape):
    return pl.BlockSpec((1,) + shape, lambda i, place: (place[0],) + (0,) * len(shape))


def gradients(place, kv, w_first, w_second, batches):
    dim, inner = w_first.shape[1:]
    sums = (batches, dim, inner)
    return pl.pallas_call(
        gradient_kernel,
        grid_spec=pltpu.PrefetchScalarGridSpec(
            num_scalar_prefetch=1,
            grid=(1,),
            in_specs=[whole(kv.shape), chosen((dim, inner)), chosen((inner, dim))],
            out_specs=[whole(sums), whole(sums)],
        ),
        out_shape=[jax.ShapeDtypeStruct(sums, f32)] * 2,
        compiler_params=pltpu.CompilerParams(vmem_limit_bytes=48 * 2**20),
        name="gradients",
    )(place, kv, w_first, w_second)


def mix_kernel(
    place_ref, kv_ref, q_ref, first_ref, second_ref, sum_first_ref, sum_second_ref, before_ref, after_ref,
    gate_ref, out_ref, keys_ref, values_ref,
):
    batches, dim, inner = sum_first_ref.shape
    part = kv_ref.shape[0] // batches
    chunk = 2 * q_ref.shape[1]
    lane = lax.broadcasted_iota(jnp.int32, (part, LANES), 1)
    left = lane < dim
    left_q = left_half(chunk // 2)
    for b in range(batches):
        rows = slice(b * part, (b + 1) * part)
        kv = kv_ref[rows, :]
        vk = half_turn(kv)
        keys_ref[rows, :] = jnp.where(left, kv, vk)
        values_ref[rows, :] = jnp.where(left, vk, jnp.where(lane == dim, 1.0, 0.0).astype(bf16))
    first, second = (first_ref[0], second_ref[0].T)
    first_ahead = first - inner_rate * before_ref[0]
    second_ahead = second - inner_rate * before_ref[1]
    first_behind = first - inner_rate * (after_ref[0] + sum_first_ref[batches - 1])
    second_behind = second - inner_rate * (after_ref[1] + sum_second_ref[batches - 1])
    gates = jnp.tanh(gate_ref[0])
    for b in range(batches):
        pieces = []
        for i in range(part // chunk):
            x = q_ref[b * (part // chunk) + i]
            turned = half_turn(x)
            pieces += [jnp.where(left_q, x, turned), jnp.where(left_q, turned, x)]
        qq = jnp.concatenate(pieces, axis=0)
        q = qq.astype(f32)
        result = (gates[0:1] + gates[1:2]) * q[:, :dim]
        ahead = (first_ahead - inner_rate * sum_first_ref[b], second_ahead - inner_rate * sum_second_ref[b])
        if b == 0:
            behind = (first_behind, second_behind)
        else:
            behind = (
                first_behind + inner_rate * sum_first_ref[b - 1],
                second_behind + inner_rate * sum_second_ref[b - 1],
            )
        for way, (a, c) in enumerate((ahead, behind)):
            z = dot(qq, jnp.concatenate(split(a), axis=0), NN)
            u = project(split(gelu(z)), centred(c))
            result = result + gates[way : way + 1] * (u * norm_scale(u))
        scaled = q * (LOG2E * dim**-0.5)
        high = scaled.astype(bf16)
        low = (scaled - high.astype(f32)).astype(bf16)
        scores = dot(jnp.where(left, high, low), keys_ref[...], NT)
        expon = jnp.exp2(scores - jnp.max(scores, axis=1, keepdims=True)).astype(bf16)
        attended = dot(expon, values_ref[...], NN)
        result = result + attended[:, :dim] * (1.0 / attended[:, dim : dim + 1])
        out_ref[b] = jnp.concatenate([result[: part // 2], result[part // 2 :]], axis=1)


def mix(place, kv, q, w_first, w_second, sum_first, sum_second, before, after, gates):
    batches, dim, inner = sum_first.shape
    part = kv.shape[0] // batches
    return pl.pallas_call(
        mix_kernel,
        grid_spec=pltpu.PrefetchScalarGridSpec(
            num_scalar_prefetch=1,
            grid=(1,),
            in_specs=[
                whole(kv.shape),
                whole(q.shape),
                chosen((dim, inner)),
                chosen((inner, dim)),
                whole(sum_first.shape),
                whole(sum_second.shape),
                whole(before.shape),
                whole(after.shape),
                chosen((2, dim)),
            ],
            out_specs=whole((batches, part // 2, LANES)),
            scratch_shapes=[pltpu.VMEM(kv.shape, bf16), pltpu.VMEM(kv.shape, bf16)],
        ),
        out_shape=jax.ShapeDtypeStruct((batches, part // 2, LANES), f32),
        compiler_params=pltpu.CompilerParams(vmem_limit_bytes=56 * 2**20),
        name="mix",
    )(place, kv, q, w_first, w_second, sum_first, sum_second, before, after, gates)


def unpack_kernel(packed_ref, out_ref):
    half = packed_ref.shape[1]
    left = left_half(half)
    for pair in range(out_ref.shape[1] // LANES):
        even = packed_ref[2 * pair].astype(f32)
        odd = packed_ref[2 * pair + 1].astype(f32)
        cols = slice(pair * LANES, (pair + 1) * LANES)
        out_ref[:half, cols] = jnp.where(left, even, half_turn(odd))
        out_ref[half:, cols] = jnp.where(left, half_turn(even), odd)


def unpack(packed, heads_here):
    return pl.pallas_call(
        unpack_kernel,
        out_shape=jax.ShapeDtypeStruct((2 * packed.shape[1], heads_here * HEAD_DIM), f32),
        compiler_params=pltpu.CompilerParams(allow_input_fusion=[True]),
        name="unpack",
    )(packed)


def on_device(queries, key_rows, value_rows, w_first, w_second, gate_pairs):
    seg, sides = (lax.axis_size("seg"), lax.axis_size("head"))
    heads_here = w_first.shape[0]
    segments = seg // GROUP
    assert heads_here <= GROUP
    both = [[s * GROUP * sides + i for i in range(GROUP * sides)] for s in range(segments)]
    lines = [[s * GROUP + i for i in range(GROUP)] for s in range(segments)]
    kv, q = pack(queries, key_rows, value_rows, heads_here, sides)
    kv = lax.all_to_all(kv, ("seg", "head"), 0, 0, tiled=True, axis_index_groups=both)
    q = lax.all_to_all(q, ("seg", "head"), 0, 0, tiled=True, axis_index_groups=both)
    kv = kv.reshape(-1, LANES)
    place = jnp.minimum(lax.axis_index("seg") % GROUP, heads_here - 1).astype(jnp.int32).reshape(1)
    sum_first, sum_second = gradients(place, kv, w_first, w_second, GROUP)
    before = after = jnp.zeros((2,) + sum_first.shape[1:], f32)
    if segments > 1:
        across = [[s * GROUP + i for s in range(segments)] for i in range(GROUP)]
        here = lax.axis_index("seg") // GROUP
        totals = lax.all_gather(
            jnp.stack([sum_first[-1], sum_second[-1]]), "seg", axis_index_groups=across
        )
        order = jnp.arange(segments).reshape(-1, 1, 1, 1)
        before = jnp.sum(jnp.where(order < here, totals, 0.0), axis=0)
        after = jnp.sum(jnp.where(order > here, totals, 0.0), axis=0)
    gates = gate_pairs.reshape(2, heads_here, HEAD_DIM).transpose(1, 0, 2)
    out = mix(place, kv, q, w_first, w_second, sum_first, sum_second, before, after, gates)
    out = lax.all_to_all(out, "seg", 0, 0, tiled=True, axis_index_groups=lines)
    return unpack(out, heads_here)


def solution(mesh):
    in_specs = (
        P(("seg", "head"), None),
        P(("seg", "head"), None),
        P(("seg", "head"), None),
        P("head", None, None),
        P("head", None, None),
        P(None, "head"),
    )
    return jax.shard_map(
        on_device, mesh=mesh, in_specs=in_specs, out_specs=P("seg", "head"), check_vma=False
    )
```

```python
import functools

import jax
import jax.numpy as jnp
from jax import lax
from jax.experimental import pallas as pl
from jax.experimental.pallas import tpu as pltpu
from jax.sharding import PartitionSpec as P

HEAD_DIM = 64
GROUP = 8
LANES = 2 * HEAD_DIM

inner_rate = 0.05
norm_epsilon = 1e-05
LOG2E = 1.4426950408889634
GELU_A = 0.7978845608028654
GELU_B = 0.044715

f32, bf16 = (jnp.float32, jnp.bfloat16)
NN = (((1,), (0,)), ((), ()))
NT = (((1,), (1,)), ((), ()))
TN = (((0,), (0,)), ((), ()))


def dot(a, b, dims):
    return lax.dot_general(a, b, dims, preferred_element_type=f32)


def split(x):
    high = x.astype(bf16)
    return high, (x - high.astype(f32)).astype(bf16)


def half_turn(x):
    return jnp.concatenate([x[:, HEAD_DIM:], x[:, :HEAD_DIM]], axis=1)


def left_half(rows):
    return lax.broadcasted_iota(jnp.int32, (rows, LANES), 1) < HEAD_DIM


def gelu(z):
    t = jnp.tanh(z * (GELU_A + (GELU_A * GELU_B) * (z * z)))
    half = 0.5 * z
    return half + half * t


def gelu_and_slope(z):
    z2 = z * z
    t = jnp.tanh(z * (GELU_A + (GELU_A * GELU_B) * z2))
    a = 0.5 + 0.5 * t
    return z * a, a + z * (2 * GELU_A + (6 * GELU_A * GELU_B) * z2) * (a * (1 - a))


def centred(second):
    return second - jnp.mean(second, axis=0, keepdims=True)


def project(hidden, second):
    high, low = hidden
    second_high, second_low = split(second)
    return dot(high, second_high, NT) + dot(high, second_low, NT) + dot(low, second_high, NT)


def norm_scale(u):
    return lax.rsqrt(jnp.mean(u * u, axis=1, keepdims=True) + norm_epsilon)


def pack_kernel(q_ref, k_ref, v_ref, out_ref, *, heads_here, sides):
    rows, width = q_ref.shape
    left = left_half(rows)
    left_q = left_half(rows // 2)
    for pair in range(width // LANES):
        cols = slice(pair * LANES, (pair + 1) * LANES)
        k, v, q = (k_ref[:, cols], v_ref[:, cols], q_ref[:, cols])
        k_turned, v_turned = (half_turn(k), half_turn(v))
        qa, qb = (q[: rows // 2], q[rows // 2 :])
        qa_turned, qb_turned = (half_turn(qa), half_turn(qb))
        for odd in range(2):
            head = 2 * pair + odd
            place = (head % heads_here) * sides + head // heads_here
            if odd:
                out_ref[place, :rows] = jnp.where(left, k_turned, v)
                out_ref[place, rows:] = jnp.where(left_q, qa_turned, qb)
            else:
                out_ref[place, :rows] = jnp.where(left, k, v_turned)
                out_ref[place, rows:] = jnp.where(left_q, qa, qb_turned)
    for place in range(heads_here * sides, out_ref.shape[0]):
        out_ref[place] = jnp.zeros(out_ref.shape[1:], bf16)


def pack(queries, key_rows, value_rows, heads_here, sides):
    rows = queries.shape[0]
    return pl.pallas_call(
        functools.partial(pack_kernel, heads_here=heads_here, sides=sides),
        out_shape=jax.ShapeDtypeStruct((GROUP * sides, rows + rows // 2, LANES), bf16),
        name="pack",
    )(queries, key_rows, value_rows)


def head_kernel(place_ref, x_ref, first_ref, second_ref, gate_ref, *rest, totals_only, across):
    if across:
        before_ref, after_ref, *rest = rest
    out_ref, keys_ref, values_ref, sum_first_ref, sum_second_ref = rest
    batches = GROUP
    dim, inner = first_ref.shape[1:]
    shards = x_ref.shape[0] // batches
    rows = x_ref.shape[1] * 2 // 3
    part = shards * rows
    lane = lax.broadcasted_iota(jnp.int32, (part, LANES), 1)
    left = lane < dim
    left_q = left_half(rows // 2)
    first, second = (first_ref[0], second_ref[0])

    first_pair = jnp.concatenate(split(first), axis=0)
    second_centred = centred(second)
    second_high, second_low = split(second)
    second_triple = jnp.concatenate([second_high, second_low, second_high], axis=0)
    sum_first = jnp.zeros((dim, inner), f32)
    sum_second = jnp.zeros((dim, inner), f32)
    for b in range(batches):
        kv = x_ref[b * shards : (b + 1) * shards, :rows].reshape(part, LANES)
        vk = half_turn(kv)
        kk = jnp.where(left, kv, vk)
        here = slice(b * part, (b + 1) * part)
        keys_ref[here, :] = kk
        values_ref[here, :] = jnp.where(left, vk, jnp.where(lane == dim, 1.0, 0.0).astype(bf16))
        k, v = (kv[:, :dim], vk[:, :dim])
        hidden, slope = gelu_and_slope(dot(kk, first_pair, NN))
        h_high, h_low = split(hidden)
        u = project((h_high, h_low), second_centred)
        r = norm_scale(u)
        n = u * r
        error = n - v.astype(f32) + k.astype(f32)
        du = (r * (1.0 / part)) * (
            error
            - jnp.mean(error, axis=1, keepdims=True)
            - n * jnp.mean(error * n, axis=1, keepdims=True)
        )
        du_high, du_low = split(du)
        sum_second = sum_second + (
            dot(du_high, h_high, TN) + dot(du_low, h_high, TN) + dot(du_high, h_low, TN)
        )
        dh = dot(jnp.concatenate([du_high, du_high, du_low], axis=1), second_triple, NN)
        dz_high, dz_low = split(dh * slope)
        sum_first = sum_first + (dot(k, dz_high, TN) + dot(k, dz_low, TN))
        sum_first_ref[b] = sum_first
        sum_second_ref[b] = sum_second
    if totals_only:
        out_ref[0] = sum_first
        out_ref[1] = sum_second
        return

    first_ahead = first_behind = first
    second_ahead = second_behind = second
    if across:
        first_ahead = first - inner_rate * before_ref[0]
        second_ahead = second - inner_rate * before_ref[1]
        first_behind = first - inner_rate * after_ref[0]
        second_behind = second - inner_rate * after_ref[1]
    first_behind = first_behind - inner_rate * sum_first
    second_behind = second_behind - inner_rate * sum_second
    gates = gate_ref[:, :dim]
    for other in range(1, gate_ref.shape[1] // dim):
        gates = jnp.where(place_ref[0] == other, gate_ref[:, other * dim : (other + 1) * dim], gates)
    gates = jnp.tanh(gates)
    for b in range(batches):
        pieces = []
        for i in range(shards):
            x = x_ref[b * shards + i, rows:]
            turned = half_turn(x)
            pieces += [jnp.where(left_q, x, turned), jnp.where(left_q, turned, x)]
        qq = jnp.concatenate(pieces, axis=0)
        q = qq.astype(f32)
        result = (gates[0:1] + gates[1:2]) * q[:, :dim]
        ahead = (first_ahead - inner_rate * sum_first_ref[b], second_ahead - inner_rate * sum_second_ref[b])
        behind = (first_behind, second_behind)
        if b > 0:
            behind = (
                first_behind + inner_rate * sum_first_ref[b - 1],
                second_behind + inner_rate * sum_second_ref[b - 1],
            )
        for way, (a, c) in enumerate((ahead, behind)):
            z = dot(qq, jnp.concatenate(split(a), axis=0), NN)
            u = project(split(gelu(z)), centred(c))
            result = result + gates[way : way + 1] * (u * norm_scale(u))
        scaled = q * (LOG2E * dim**-0.5)
        high = scaled.astype(bf16)
        low = (scaled - high.astype(f32)).astype(bf16)
        scores = dot(jnp.where(left, high, low), keys_ref[...], NT)
        expon = jnp.exp2(scores - jnp.max(scores, axis=1, keepdims=True)).astype(bf16)
        attended = dot(expon, values_ref[...], NN)
        result = result + attended[:, :dim] * (1.0 / attended[:, dim : dim + 1])
        out_ref[b] = jnp.concatenate([result[: part // 2], result[part // 2 :]], axis=1)


def whole(shape):
    return pl.BlockSpec(shape, lambda i, place: (0,) * len(shape))


def chosen(shape):
    return pl.BlockSpec((1,) + shape, lambda i, place: (place[0],) + (0,) * len(shape))


def work_on_head(place, x, w_first, w_second, gate_pairs, others=(), totals_only=False):
    weights = w_first.shape[1:]
    tokens = x.shape[0] * (x.shape[1] * 2 // 3)
    out = (2,) + weights if totals_only else (GROUP, tokens // GROUP // 2, LANES)
    return pl.pallas_call(
        functools.partial(head_kernel, totals_only=totals_only, across=len(others) > 0),
        grid_spec=pltpu.PrefetchScalarGridSpec(
            num_scalar_prefetch=1,
            grid=(1,),
            in_specs=[whole(x.shape), chosen(weights), chosen(weights), whole(gate_pairs.shape)]
            + [whole(other.shape) for other in others],
            out_specs=whole(out),
            scratch_shapes=[pltpu.VMEM((tokens, LANES), bf16)] * 2
            + [pltpu.VMEM((GROUP,) + weights, f32)] * 2,
        ),
        out_shape=jax.ShapeDtypeStruct(out, f32),
        compiler_params=pltpu.CompilerParams(vmem_limit_bytes=56 * 2**20),
        name="totals" if totals_only else "head",
    )(place, x, w_first, w_second, gate_pairs, *others)


def unpack_kernel(packed_ref, out_ref):
    half = packed_ref.shape[1]
    left = left_half(half)
    for pair in range(out_ref.shape[1] // LANES):
        even = packed_ref[2 * pair].astype(f32)
        odd = packed_ref[2 * pair + 1].astype(f32)
        cols = slice(pair * LANES, (pair + 1) * LANES)
        out_ref[:half, cols] = jnp.where(left, even, half_turn(odd))
        out_ref[half:, cols] = jnp.where(left, half_turn(even), odd)


def unpack(packed, heads_here):
    return pl.pallas_call(
        unpack_kernel,
        out_shape=jax.ShapeDtypeStruct((2 * packed.shape[1], heads_here * HEAD_DIM), f32),
        compiler_params=pltpu.CompilerParams(allow_input_fusion=[True]),
        name="unpack",
    )(packed)


def on_device(queries, key_rows, value_rows, w_first, w_second, gate_pairs):
    seg, sides = (lax.axis_size("seg"), lax.axis_size("head"))
    heads_here = w_first.shape[0]
    segments = seg // GROUP
    assert heads_here <= GROUP
    both = [[s * GROUP * sides + i for i in range(GROUP * sides)] for s in range(segments)]
    lines = [[s * GROUP + i for i in range(GROUP)] for s in range(segments)]
    w_second = jnp.swapaxes(w_second, 1, 2)
    x = pack(queries, key_rows, value_rows, heads_here, sides)
    x = lax.all_to_all(x, ("seg", "head"), 0, 0, tiled=True, axis_index_groups=both)
    place = jnp.minimum(lax.axis_index("seg") % GROUP, heads_here - 1).astype(jnp.int32).reshape(1)
    others = ()
    if segments > 1:
        totals = work_on_head(place, x, w_first, w_second, gate_pairs, totals_only=True)
        across = [[s * GROUP + i for s in range(segments)] for i in range(GROUP)]
        here = lax.axis_index("seg") // GROUP
        totals = lax.all_gather(totals, "seg", axis_index_groups=across)
        order = jnp.arange(segments).reshape(-1, 1, 1, 1)
        before = jnp.sum(jnp.where(order < here, totals, 0.0), axis=0)
        after = jnp.sum(jnp.where(order > here, totals, 0.0), axis=0)
        others = (before, after)
    out = work_on_head(place, x, w_first, w_second, gate_pairs, others)
    out = lax.all_to_all(out, "seg", 0, 0, tiled=True, axis_index_groups=lines)
    return unpack(out, heads_here)


def solution(mesh):
    in_specs = (
        P(("seg", "head"), None),
        P(("seg", "head"), None),
        P(("seg", "head"), None),
        P("head", None, None),
        P("head", None, None),
        P(None, "head"),
    )
    return jax.shard_map(
        on_device, mesh=mesh, in_specs=in_specs, out_specs=P("seg", "head"), check_vma=False
    )
```

```python
import functools

import jax
import jax.numpy as jnp
from jax import lax
from jax.experimental import pallas as pl
from jax.experimental.pallas import tpu as pltpu
from jax.sharding import PartitionSpec as P

HEAD_DIM = 64
GROUP = 8
LANES = 2 * HEAD_DIM

inner_rate = 0.05
norm_epsilon = 1e-05
LOG2E = 1.4426950408889634
GELU_A = 0.7978845608028654
GELU_B = 0.044715

f32, bf16 = (jnp.float32, jnp.bfloat16)
NN = (((1,), (0,)), ((), ()))
NT = (((1,), (1,)), ((), ()))
TN = (((0,), (0,)), ((), ()))


def dot(a, b, dims):
    return lax.dot_general(a, b, dims, preferred_element_type=f32)


def split(x):
    high = x.astype(bf16)
    return high, (x - high.astype(f32)).astype(bf16)


def half_turn(x):
    return jnp.concatenate([x[:, HEAD_DIM:], x[:, :HEAD_DIM]], axis=1)


def left_half(rows):
    return lax.broadcasted_iota(jnp.int32, (rows, LANES), 1) < HEAD_DIM


def gelu(z):
    t = jnp.tanh(z * (GELU_A + (GELU_A * GELU_B) * (z * z)))
    half = 0.5 * z
    return half + half * t


def gelu_and_slope(z):
    z2 = z * z
    t = jnp.tanh(z * (GELU_A + (GELU_A * GELU_B) * z2))
    a = 0.5 + 0.5 * t
    return z * a, a + z * (2 * GELU_A + (6 * GELU_A * GELU_B) * z2) * (a * (1 - a))


def centred(second):
    return second - jnp.mean(second, axis=0, keepdims=True)


def project(hidden, second):
    high, low = hidden
    second_high, second_low = split(second)
    return dot(high, second_high, NT) + dot(high, second_low, NT) + dot(low, second_high, NT)


def norm_scale(u):
    return lax.rsqrt(jnp.mean(u * u, axis=1, keepdims=True) + norm_epsilon)


def pack_kernel(q_ref, k_ref, v_ref, out_ref, *, heads_here, sides):
    rows, width = q_ref.shape
    left = left_half(rows)
    left_q = left_half(rows // 2)
    for pair in range(width // LANES):
        cols = slice(pair * LANES, (pair + 1) * LANES)
        k, v, q = (k_ref[:, cols], v_ref[:, cols], q_ref[:, cols])
        k_turned, v_turned = (half_turn(k), half_turn(v))
        qa, qb = (q[: rows // 2], q[rows // 2 :])
        qa_turned, qb_turned = (half_turn(qa), half_turn(qb))
        for odd in range(2):
            head = 2 * pair + odd
            place = (head % heads_here) * sides + head // heads_here
            if odd:
                out_ref[place, :rows] = jnp.where(left, k_turned, v)
                out_ref[place, rows:] = jnp.where(left_q, qa_turned, qb)
            else:
                out_ref[place, :rows] = jnp.where(left, k, v_turned)
                out_ref[place, rows:] = jnp.where(left_q, qa, qb_turned)
    for place in range(heads_here * sides, out_ref.shape[0]):
        out_ref[place] = jnp.zeros(out_ref.shape[1:], bf16)


def pack(queries, key_rows, value_rows, heads_here, sides):
    rows = queries.shape[0]
    return pl.pallas_call(
        functools.partial(pack_kernel, heads_here=heads_here, sides=sides),
        out_shape=jax.ShapeDtypeStruct((GROUP * sides, rows + rows // 2, LANES), bf16),
        name="pack",
    )(queries, key_rows, value_rows)


def head_kernel(place_ref, x_ref, first_ref, second_ref, gate_ref, *rest, totals_only, across):
    if across:
        before_ref, after_ref, *rest = rest
    out_ref, keys_ref, values_ref, sum_first_ref, sum_second_ref = rest
    batches = GROUP
    dim, inner = first_ref.shape[1:]
    shards = x_ref.shape[0] // batches
    rows = x_ref.shape[1] * 2 // 3
    part = shards * rows
    lane = lax.broadcasted_iota(jnp.int32, (part, LANES), 1)
    left = lane < dim
    left_q = left_half(rows // 2)
    first, second = (first_ref[0], second_ref[0])

    first_pair = jnp.concatenate(split(first), axis=0)
    second_centred = centred(second)
    second_high, second_low = split(second)
    second_triple = jnp.concatenate([second_high, second_low, second_high], axis=0)
    sum_first = jnp.zeros((dim, inner), f32)
    sum_second = jnp.zeros((dim, inner), f32)
    for b in range(batches):
        kv = x_ref[b * shards : (b + 1) * shards, :rows].reshape(part, LANES)
        vk = half_turn(kv)
        kk = jnp.where(left, kv, vk)
        here = slice(b * part, (b + 1) * part)
        keys_ref[here, :] = kk
        values_ref[here, :] = jnp.where(left, vk, jnp.where(lane == dim, 1.0, 0.0).astype(bf16))
        k, v = (kv[:, :dim], vk[:, :dim])
        hidden, slope = gelu_and_slope(dot(kk, first_pair, NN))
        h_high, h_low = split(hidden)
        u = project((h_high, h_low), second_centred)
        r = norm_scale(u)
        n = u * r
        error = n - v.astype(f32) + k.astype(f32)
        du = (r * (1.0 / part)) * (
            error
            - jnp.mean(error, axis=1, keepdims=True)
            - n * jnp.mean(error * n, axis=1, keepdims=True)
        )
        du_high, du_low = split(du)
        sum_second = sum_second + (
            dot(du_high, h_high, TN) + dot(du_low, h_high, TN) + dot(du_high, h_low, TN)
        )
        dh = dot(jnp.concatenate([du_high, du_high, du_low], axis=1), second_triple, NN)
        dz_high, dz_low = split(dh * slope)
        sum_first = sum_first + (dot(k, dz_high, TN) + dot(k, dz_low, TN))
        sum_first_ref[b] = sum_first
        sum_second_ref[b] = sum_second
    if totals_only:
        out_ref[0] = sum_first
        out_ref[1] = sum_second
        return

    first_ahead = first_behind = first
    second_ahead = second_behind = second
    if across:
        first_ahead = first - inner_rate * before_ref[0]
        second_ahead = second - inner_rate * before_ref[1]
        first_behind = first - inner_rate * after_ref[0]
        second_behind = second - inner_rate * after_ref[1]
    first_behind = first_behind - inner_rate * sum_first
    second_behind = second_behind - inner_rate * sum_second
    gates = gate_ref[:, :dim]
    for other in range(1, gate_ref.shape[1] // dim):
        gates = jnp.where(place_ref[0] == other, gate_ref[:, other * dim : (other + 1) * dim], gates)
    gates = jnp.tanh(gates)
    for b in range(batches):
        pieces = []
        for i in range(shards):
            x = x_ref[b * shards + i, rows:]
            turned = half_turn(x)
            pieces += [jnp.where(left_q, x, turned), jnp.where(left_q, turned, x)]
        qq = jnp.concatenate(pieces, axis=0)
        q = qq.astype(f32)
        result = (gates[0:1] + gates[1:2]) * q[:, :dim]
        ahead = (first_ahead - inner_rate * sum_first_ref[b], second_ahead - inner_rate * sum_second_ref[b])
        behind = (first_behind, second_behind)
        if b > 0:
            behind = (
                first_behind + inner_rate * sum_first_ref[b - 1],
                second_behind + inner_rate * sum_second_ref[b - 1],
            )
        for way, (a, c) in enumerate((ahead, behind)):
            z = dot(qq, jnp.concatenate(split(a), axis=0), NN)
            u = project(split(gelu(z)), centred(c))
            result = result + gates[way : way + 1] * (u * norm_scale(u))
        scaled = q * (LOG2E * dim**-0.5)
        high = scaled.astype(bf16)
        low = (scaled - high.astype(f32)).astype(bf16)
        scores = dot(jnp.where(left, high, low), keys_ref[...], NT)
        expon = jnp.exp2(scores - jnp.max(scores, axis=1, keepdims=True)).astype(bf16)
        attended = dot(expon, values_ref[...], NN)
        result = result + attended[:, :dim] * (1.0 / attended[:, dim : dim + 1])
        out_ref[b] = jnp.concatenate([result[: part // 2], result[part // 2 :]], axis=1)


def whole(shape):
    return pl.BlockSpec(shape, lambda i, place: (0,) * len(shape))


def chosen(shape):
    return pl.BlockSpec((1,) + shape, lambda i, place: (place[0],) + (0,) * len(shape))


def work_on_head(place, x, w_first, w_second, gate_pairs, others=(), totals_only=False):
    weights = w_first.shape[1:]
    tokens = x.shape[0] * (x.shape[1] * 2 // 3)
    out = (2,) + weights if totals_only else (GROUP, tokens // GROUP // 2, LANES)
    return pl.pallas_call(
        functools.partial(head_kernel, totals_only=totals_only, across=len(others) > 0),
        grid_spec=pltpu.PrefetchScalarGridSpec(
            num_scalar_prefetch=1,
            grid=(1,),
            in_specs=[whole(x.shape), chosen(weights), chosen(weights), whole(gate_pairs.shape)]
            + [whole(other.shape) for other in others],
            out_specs=whole(out),
            scratch_shapes=[pltpu.VMEM((tokens, LANES), bf16)] * 2
            + [pltpu.VMEM((GROUP,) + weights, f32)] * 2,
        ),
        out_shape=jax.ShapeDtypeStruct(out, f32),
        compiler_params=pltpu.CompilerParams(vmem_limit_bytes=56 * 2**20),
        name="totals" if totals_only else "head",
    )(place, x, w_first, w_second, gate_pairs, *others)


def unpack_kernel(packed_ref, out_ref):
    half = packed_ref.shape[1]
    left = left_half(half)
    for pair in range(out_ref.shape[1] // LANES):
        even = packed_ref[2 * pair].astype(f32)
        odd = packed_ref[2 * pair + 1].astype(f32)
        cols = slice(pair * LANES, (pair + 1) * LANES)
        out_ref[:half, cols] = jnp.where(left, even, half_turn(odd))
        out_ref[half:, cols] = jnp.where(left, half_turn(even), odd)


def unpack(packed, heads_here):
    return pl.pallas_call(
        unpack_kernel,
        out_shape=jax.ShapeDtypeStruct((2 * packed.shape[1], heads_here * HEAD_DIM), f32),
        compiler_params=pltpu.CompilerParams(allow_input_fusion=[True]),
        name="unpack",
    )(packed)


def on_device(queries, key_rows, value_rows, w_first, w_second, gate_pairs):
    seg, sides = (lax.axis_size("seg"), lax.axis_size("head"))
    heads_here = w_first.shape[0]
    segments = seg // GROUP
    assert heads_here <= GROUP
    both = [[s * GROUP * sides + i for i in range(GROUP * sides)] for s in range(segments)]
    lines = [[s * GROUP + i for i in range(GROUP)] for s in range(segments)]
    w_second = jnp.swapaxes(w_second, 1, 2)
    x = pack(queries, key_rows, value_rows, heads_here, sides)
    x = lax.all_to_all(x, ("seg", "head"), 0, 0, tiled=True, axis_index_groups=both)
    place = jnp.minimum(lax.axis_index("seg") % GROUP, heads_here - 1).astype(jnp.int32).reshape(1)
    others = ()
    if segments > 1:
        totals = work_on_head(place, x, w_first, w_second, gate_pairs, totals_only=True)
        across = [[s * GROUP + i for s in range(segments)] for i in range(GROUP)]
        here = lax.axis_index("seg") // GROUP
        totals = lax.all_gather(totals, "seg", axis_index_groups=across)
        order = jnp.arange(segments).reshape(-1, 1, 1, 1)
        before = jnp.sum(jnp.where(order < here, totals, 0.0), axis=0)
        after = jnp.sum(jnp.where(order > here, totals, 0.0), axis=0)
        others = (before, after)
    out = work_on_head(place, x, w_first, w_second, gate_pairs, others)
    out = lax.all_to_all(out.astype(jnp.float16), "seg", 0, 0, tiled=True, axis_index_groups=lines).astype(f32)
    return unpack(out, heads_here)


def solution(mesh):
    in_specs = (
        P(("seg", "head"), None),
        P(("seg", "head"), None),
        P(("seg", "head"), None),
        P("head", None, None),
        P("head", None, None),
        P(None, "head"),
    )
    return jax.shard_map(
        on_device, mesh=mesh, in_specs=in_specs, out_specs=P("seg", "head"), check_vma=False
    )
```

```python
import functools

import jax
import jax.numpy as jnp
from jax import lax
from jax.experimental import pallas as pl
from jax.experimental.pallas import tpu as pltpu
from jax.sharding import PartitionSpec as P

HEAD_DIM = 64
GROUP = 8
LANES = 2 * HEAD_DIM

inner_rate = 0.05
norm_epsilon = 1e-05
LOG2E = 1.4426950408889634
BOUND = 36.0
SPREAD = 240.0
GELU_A = 0.7978845608028654
GELU_B = 0.044715

f32, bf16 = (jnp.float32, jnp.bfloat16)
NN = (((1,), (0,)), ((), ()))
NT = (((1,), (1,)), ((), ()))
TN = (((0,), (0,)), ((), ()))


in_vmem = pl.BlockSpec(memory_space=pltpu.VMEM)
in_hbm = pl.BlockSpec(memory_space=pl.ANY)


def vmem(x):
    return pltpu.with_memory_space_constraint(x, pltpu.VMEM)


def dot(a, b, dims):
    return lax.dot_general(a, b, dims, preferred_element_type=f32)


def split(x):
    high = x.astype(bf16)
    return high, (x - high.astype(f32)).astype(bf16)


def half_turn(x):
    return jnp.concatenate([x[:, HEAD_DIM:], x[:, :HEAD_DIM]], axis=1)


def left_half(rows):
    return lax.broadcasted_iota(jnp.int32, (rows, LANES), 1) < HEAD_DIM


def gelu(z):
    t = jnp.tanh(z * (GELU_A + (GELU_A * GELU_B) * (z * z)))
    half = 0.5 * z
    return half + half * t


def gelu_and_slope(z):
    z2 = z * z
    t = jnp.tanh(z * (GELU_A + (GELU_A * GELU_B) * z2))
    a = 0.5 + 0.5 * t
    return z * a, a + z * (2 * GELU_A + (6 * GELU_A * GELU_B) * z2) * (a * (1 - a))


def centred(second):
    return second - jnp.mean(second, axis=0, keepdims=True)


def project(hidden, second):
    high, low = hidden
    second_high, second_low = second
    return dot(high, second_high, NT) + dot(high, second_low, NT) + dot(low, second_high, NT)


def norm_scale(u):
    return lax.rsqrt(jnp.mean(u * u, axis=1, keepdims=True) + norm_epsilon)


def pack_kernel(q_ref, k_ref, v_ref, out_ref, *, heads_here, sides):
    rows, width = q_ref.shape
    left = left_half(rows)
    left_q = left_half(rows // 2)
    for pair in range(width // LANES):
        cols = slice(pair * LANES, (pair + 1) * LANES)
        k, v, q = (k_ref[:, cols], v_ref[:, cols], q_ref[:, cols])
        k_turned, v_turned = (half_turn(k), half_turn(v))
        qa, qb = (q[: rows // 2], q[rows // 2 :])
        qa_turned, qb_turned = (half_turn(qa), half_turn(qb))
        for odd in range(2):
            head = 2 * pair + odd
            place = (head % heads_here) * sides + head // heads_here
            if odd:
                out_ref[place, :rows] = jnp.where(left, k_turned, v)
                out_ref[place, rows:] = jnp.where(left_q, qa_turned, qb)
            else:
                out_ref[place, :rows] = jnp.where(left, k, v_turned)
                out_ref[place, rows:] = jnp.where(left_q, qa, qb_turned)
    for place in range(heads_here * sides, out_ref.shape[0]):
        out_ref[place] = jnp.zeros(out_ref.shape[1:], bf16)


def pack(queries, key_rows, value_rows, heads_here, sides):
    rows = queries.shape[0]
    return pl.pallas_call(
        functools.partial(pack_kernel, heads_here=heads_here, sides=sides),
        out_specs=in_vmem,
        out_shape=pltpu.VMEM((GROUP * sides, rows + rows // 2, LANES), bf16),
        name="pack",
    )(queries, key_rows, value_rows)


def encode(x):
    y = jnp.exp2(SPREAD * jnp.sqrt(jnp.abs(x) * (1.0 / BOUND)) - SPREAD / 2)
    return jnp.where(x < 0, -y, y).astype(bf16)


def decode(y):
    y = y.astype(f32)
    root = jnp.log2(jnp.abs(y)) * (1.0 / SPREAD) + 0.5
    x = BOUND * (root * root)
    return jnp.where(y < 0, -x, x)


def head_kernel(place_ref, x_ref, first_hbm, second_hbm, gate_hbm, *rest, totals_only, across):
    if across:
        before_ref, after_ref, *rest = rest
    out_ref, first_ref, second_ref, gate_ref, copied, *rest = rest
    keys_ref, values_ref, high_ref, low_ref, slope_ref, du_ref, attended_ref, sum_first_ref, sum_second_ref = rest
    batches = GROUP
    dim, inner = first_ref.shape
    shards = x_ref.shape[0] // batches
    rows = x_ref.shape[1] * 2 // 3
    part = shards * rows
    lane = lax.broadcasted_iota(jnp.int32, (part, LANES), 1)
    left = lane < dim
    left_q = left_half(rows // 2)

    def here(b):
        return slice(b * part, (b + 1) * part)

    copies = [
        pltpu.make_async_copy(first_hbm.at[place_ref[0]], first_ref, copied.at[0]),
        pltpu.make_async_copy(second_hbm.at[place_ref[0]], second_ref, copied.at[1]),
        pltpu.make_async_copy(gate_hbm, gate_ref, copied.at[2]),
    ]
    for copy in copies:
        copy.start()

    def lay_out(b):
        kv = x_ref[b * shards : (b + 1) * shards, :rows].reshape(part, LANES)
        vk = half_turn(kv)
        keys_ref[here(b), :] = jnp.where(left, kv, vk)
        values_ref[here(b), :] = jnp.where(left, vk, jnp.where(lane == dim, 1.0, 0.0).astype(bf16))

    def queries(b):
        pieces = []
        for i in range(shards):
            x = x_ref[b * shards + i, rows:]
            turned = half_turn(x)
            pieces += [jnp.where(left_q, x, turned), jnp.where(left_q, turned, x)]
        return jnp.concatenate(pieces, axis=0)

    def scores(b):
        scaled = queries(b).astype(f32) * (LOG2E * dim**-0.5)
        high = scaled.astype(bf16)
        low = (scaled - high.astype(f32)).astype(bf16)
        return dot(jnp.where(left, high, low), keys_ref[...], NT)

    def attend(b, score):
        expon = jnp.exp2(score - jnp.max(score, axis=1, keepdims=True)).astype(bf16)
        attended = dot(expon, values_ref[...], NN)
        attended_ref[here(b), :] = attended[:, :dim] * (1.0 / attended[:, dim : dim + 1])

    for b in range(batches):
        lay_out(b)
    score = None if totals_only else scores(0)
    for copy in copies:
        copy.wait()
    first, second = (first_ref[...], second_ref[...])
    first_pair = jnp.concatenate(split(first), axis=0)
    second_centred = split(centred(second))
    second_high, second_low = split(second)
    second_triple = jnp.concatenate([second_high, second_low, second_high], axis=0)

    def hidden(b):
        h, slope = gelu_and_slope(dot(keys_ref[here(b), :], first_pair, NN))
        high_ref[here(b), :], low_ref[here(b), :] = split(h)
        slope_ref[here(b), :] = slope

    def error(b):
        u = project((high_ref[here(b), :], low_ref[here(b), :]), second_centred)
        r = norm_scale(u)
        n = u * r
        e = n - (values_ref[here(b), :dim].astype(f32) - keys_ref[here(b), :dim].astype(f32))
        du = (r * (1.0 / part)) * (
            e - jnp.mean(e, axis=1, keepdims=True) - n * jnp.mean(e * n, axis=1, keepdims=True)
        )
        du_high, du_low = split(du)
        du_ref[here(b), :] = jnp.concatenate([du_high, du_high, du_low], axis=1)

    def add_gradient(b, sums):
        du = du_ref[here(b), :]
        du_high, du_low = (du[:, :dim], du[:, 2 * dim :])
        h_high, h_low = (high_ref[here(b), :], low_ref[here(b), :])
        grad_second = dot(du_high, h_high, TN) + dot(du_low, h_high, TN) + dot(du_high, h_low, TN)
        dz_high, dz_low = split(dot(du, second_triple, NN) * slope_ref[here(b), :])
        k = keys_ref[here(b), :dim]
        sums = (sums[0] + (dot(k, dz_high, TN) + dot(k, dz_low, TN)), sums[1] + grad_second)
        sum_first_ref[b], sum_second_ref[b] = sums
        return sums

    sums = (jnp.zeros((dim, inner), f32), jnp.zeros((dim, inner), f32))
    for step in range(batches + 2):
        if step < batches:
            hidden(step)
        if step + 1 < batches and not totals_only:
            next_score = scores(step + 1)
        if 1 <= step < batches + 1:
            error(step - 1)
        if step < batches and not totals_only:
            attend(step, score)
            score = next_score
        if step >= 2:
            sums = add_gradient(step - 2, sums)
    if totals_only:
        out_ref[0], out_ref[1] = sums
        return

    starts = [[first, second], [first - inner_rate * sums[0], second - inner_rate * sums[1]]]
    if across:
        for way, other in enumerate((before_ref, after_ref)):
            for i in range(2):
                starts[way][i] = starts[way][i] - inner_rate * other[i]
    gates = gate_ref[:, :dim]
    for other in range(1, gate_ref.shape[1] // dim):
        gates = jnp.where(place_ref[0] == other, gate_ref[:, other * dim : (other + 1) * dim], gates)
    gates = jnp.tanh(gates)

    def enter_model(b, way):
        w, v = starts[way]
        if way == 0:
            w, v = (w - inner_rate * sum_first_ref[b], v - inner_rate * sum_second_ref[b])
        elif b > 0:
            w, v = (w + inner_rate * sum_first_ref[b - 1], v + inner_rate * sum_second_ref[b - 1])
        z = dot(queries(b), jnp.concatenate(split(w), axis=0), NN)
        return split(gelu(z)), split(centred(v))

    def leave_model(way, entered):
        u = project(*entered)
        return gates[way : way + 1] * (u * norm_scale(u))

    ahead, behind = (enter_model(0, 0), enter_model(0, 1))
    for b in range(batches):
        last = b + 1 == batches
        next_ahead = None if last else enter_model(b + 1, 0)
        result = leave_model(0, ahead)
        next_behind = None if last else enter_model(b + 1, 1)
        result = result + leave_model(1, behind)
        q = queries(b)[:, :dim].astype(f32)
        result = encode(attended_ref[here(b), :] + (gates[0:1] + gates[1:2]) * q + result)
        out_ref[b] = jnp.concatenate([result[: part // 2], result[part // 2 :]], axis=1)
        ahead, behind = (next_ahead, next_behind)


def work_on_head(place, x, w_first, w_second, gate_pairs, others=(), totals_only=False):
    dim, inner = w_first.shape[1:]
    tokens = x.shape[0] * (x.shape[1] * 2 // 3)
    if totals_only:
        out = pltpu.VMEM((2, dim, inner), f32)
    else:
        out = pltpu.VMEM((GROUP, tokens // GROUP // 2, LANES), bf16)
    return pl.pallas_call(
        functools.partial(head_kernel, totals_only=totals_only, across=len(others) > 0),
        grid_spec=pltpu.PrefetchScalarGridSpec(
            num_scalar_prefetch=1,
            grid=(1,),
            in_specs=[in_vmem] + [in_hbm] * 3 + [in_vmem] * len(others),
            out_specs=in_vmem,
            scratch_shapes=[
                pltpu.VMEM((dim, inner), f32),
                pltpu.VMEM((dim, inner), f32),
                pltpu.VMEM(gate_pairs.shape, f32),
                pltpu.SemaphoreType.DMA((3,)),
                pltpu.VMEM((tokens, LANES), bf16),
                pltpu.VMEM((tokens, LANES), bf16),
                pltpu.VMEM((tokens, inner), bf16),
                pltpu.VMEM((tokens, inner), bf16),
                pltpu.VMEM((tokens, inner), f32),
                pltpu.VMEM((tokens, 3 * dim), bf16),
                pltpu.VMEM((tokens, dim), f32),
                pltpu.VMEM((GROUP, dim, inner), f32),
                pltpu.VMEM((GROUP, dim, inner), f32),
            ],
        ),
        out_shape=out,
        compiler_params=pltpu.CompilerParams(vmem_limit_bytes=52 * 2**20),
        name="totals" if totals_only else "head",
    )(place, vmem(x), w_first, w_second, gate_pairs, *[vmem(other) for other in others])


def unpack_kernel(packed_ref, out_ref):
    half = packed_ref.shape[1]
    left = left_half(half)
    for pair in range(out_ref.shape[1] // LANES):
        even = packed_ref[2 * pair]
        odd = packed_ref[2 * pair + 1]
        cols = slice(pair * LANES, (pair + 1) * LANES)
        out_ref[:half, cols] = decode(jnp.where(left, even, half_turn(odd)))
        out_ref[half:, cols] = decode(jnp.where(left, half_turn(even), odd))


def unpack(packed, heads_here):
    return pl.pallas_call(
        unpack_kernel,
        in_specs=[in_vmem],
        out_shape=jax.ShapeDtypeStruct((2 * packed.shape[1], heads_here * HEAD_DIM), f32),
        name="unpack",
    )(vmem(packed))


def on_device(queries, key_rows, value_rows, w_first, w_second, gate_pairs):
    seg, sides = (lax.axis_size("seg"), lax.axis_size("head"))
    heads_here = w_first.shape[0]
    segments = seg // GROUP
    assert heads_here <= GROUP
    both = [[s * GROUP * sides + i for i in range(GROUP * sides)] for s in range(segments)]
    lines = [[s * GROUP + i for i in range(GROUP)] for s in range(segments)]
    w_second = jnp.swapaxes(w_second, 1, 2)
    x = pack(queries, key_rows, value_rows, heads_here, sides)
    x = lax.all_to_all(x, ("seg", "head"), 0, 0, tiled=True, axis_index_groups=both)
    place = jnp.minimum(lax.axis_index("seg") % GROUP, heads_here - 1).astype(jnp.int32).reshape(1)
    others = ()
    if segments > 1:
        totals = work_on_head(place, x, w_first, w_second, gate_pairs, totals_only=True)
        across = [[s * GROUP + i for s in range(segments)] for i in range(GROUP)]
        here = lax.axis_index("seg") // GROUP
        totals = lax.all_gather(totals, "seg", axis_index_groups=across)
        order = jnp.arange(segments).reshape(-1, 1, 1, 1)
        before = jnp.sum(jnp.where(order < here, totals, 0.0), axis=0)
        after = jnp.sum(jnp.where(order > here, totals, 0.0), axis=0)
        others = (before, after)
    out = work_on_head(place, x, w_first, w_second, gate_pairs, others)
    out = lax.all_to_all(out, "seg", 0, 0, tiled=True, axis_index_groups=lines)
    return unpack(out, heads_here)


def solution(mesh):
    in_specs = (
        P(("seg", "head"), None),
        P(("seg", "head"), None),
        P(("seg", "head"), None),
        P("head", None, None),
        P("head", None, None),
        P(None, "head"),
    )
    return jax.shard_map(
        on_device, mesh=mesh, in_specs=in_specs, out_specs=P("seg", "head"), check_vma=False
    )
```

```python
import functools

import jax
import jax.numpy as jnp
from jax import lax
from jax.experimental import pallas as pl
from jax.experimental.pallas import tpu as pltpu
from jax.sharding import PartitionSpec as P

HEAD_DIM = 64
GROUP = 8
LANES = 2 * HEAD_DIM

inner_rate = 0.05
norm_epsilon = 1e-05
LOG2E = 1.4426950408889634
BOUND = 36.0
SPREAD = 240.0
GELU_A = 0.7978845608028654
GELU_B = 0.044715

f32, bf16 = (jnp.float32, jnp.bfloat16)
NN = (((1,), (0,)), ((), ()))
NT = (((1,), (1,)), ((), ()))
TN = (((0,), (0,)), ((), ()))


in_vmem = pl.BlockSpec(memory_space=pltpu.VMEM)
in_hbm = pl.BlockSpec(memory_space=pltpu.HBM)


def hbm(x):
    return pltpu.with_memory_space_constraint(x, pltpu.HBM)


def vmem(x):
    return pltpu.with_memory_space_constraint(x, pltpu.VMEM)


def dot(a, b, dims):
    return lax.dot_general(a, b, dims, preferred_element_type=f32)


def split(x):
    high = x.astype(bf16)
    return high, (x - high.astype(f32)).astype(bf16)


def half_turn(x):
    return jnp.concatenate([x[:, HEAD_DIM:], x[:, :HEAD_DIM]], axis=1)


def left_half(rows):
    return lax.broadcasted_iota(jnp.int32, (rows, LANES), 1) < HEAD_DIM


def gelu(z):
    t = jnp.tanh(z * (GELU_A + (GELU_A * GELU_B) * (z * z)))
    half = 0.5 * z
    return half + half * t


def gelu_and_slope(z):
    z2 = z * z
    t = jnp.tanh(z * (GELU_A + (GELU_A * GELU_B) * z2))
    a = 0.5 + 0.5 * t
    return z * a, a + z * (2 * GELU_A + (6 * GELU_A * GELU_B) * z2) * (a * (1 - a))


def centred(second):
    return second - jnp.mean(second, axis=0, keepdims=True)


def project(hidden, second):
    high, low = hidden
    second_high, second_low = second
    return dot(high, second_high, NT) + dot(high, second_low, NT) + dot(low, second_high, NT)


def norm_scale(u):
    return lax.rsqrt(jnp.mean(u * u, axis=1, keepdims=True) + norm_epsilon)


def pack_kernel(q_ref, k_ref, v_ref, out_ref, *, heads_here, sides):
    rows, width = q_ref.shape
    left = left_half(rows)
    left_q = left_half(rows // 2)
    for pair in range(width // LANES):
        cols = slice(pair * LANES, (pair + 1) * LANES)
        k, v, q = (k_ref[:, cols], v_ref[:, cols], q_ref[:, cols])
        k_turned, v_turned = (half_turn(k), half_turn(v))
        qa, qb = (q[: rows // 2], q[rows // 2 :])
        qa_turned, qb_turned = (half_turn(qa), half_turn(qb))
        for odd in range(2):
            head = 2 * pair + odd
            place = (head % heads_here) * sides + head // heads_here
            if odd:
                out_ref[place, :rows] = jnp.where(left, k_turned, v)
                out_ref[place, rows:] = jnp.where(left_q, qa_turned, qb)
            else:
                out_ref[place, :rows] = jnp.where(left, k, v_turned)
                out_ref[place, rows:] = jnp.where(left_q, qa, qb_turned)
    for place in range(heads_here * sides, out_ref.shape[0]):
        out_ref[place] = jnp.zeros(out_ref.shape[1:], bf16)


def pack(queries, key_rows, value_rows, heads_here, sides):
    rows = queries.shape[0]
    return pl.pallas_call(
        functools.partial(pack_kernel, heads_here=heads_here, sides=sides),
        out_specs=in_vmem,
        out_shape=pltpu.VMEM((GROUP * sides, rows + rows // 2, LANES), bf16),
        name="pack",
    )(queries, key_rows, value_rows)


def encode(x):
    y = jnp.exp2(SPREAD * jnp.sqrt(jnp.abs(x) * (1.0 / BOUND)) - SPREAD / 2)
    return jnp.where(x < 0, -y, y).astype(bf16)


def decode(y):
    y = y.astype(f32)
    root = jnp.log2(jnp.abs(y)) * (1.0 / SPREAD) + 0.5
    x = BOUND * (root * root)
    return jnp.where(y < 0, -x, x)


def head_kernel(x_ref, first_hbm, second_hbm, gate_hbm, *rest, totals_only, across):
    if across:
        before_ref, after_ref, *rest = rest
    out_ref, first_ref, second_ref, gate_ref, copied, *rest = rest
    keys_ref, values_ref, high_ref, low_ref, slope_ref, du_ref, attended_ref, sum_first_ref, sum_second_ref = rest
    batches = GROUP
    dim, inner = first_ref.shape
    place = jnp.minimum(lax.axis_index("seg") % GROUP, first_hbm.shape[0] - 1)
    shards = x_ref.shape[0] // batches
    rows = x_ref.shape[1] * 2 // 3
    part = shards * rows
    lane = lax.broadcasted_iota(jnp.int32, (part, LANES), 1)
    left = lane < dim
    left_q = left_half(rows // 2)

    def here(b):
        return slice(b * part, (b + 1) * part)

    copies = [
        pltpu.make_async_copy(first_hbm.at[place], first_ref, copied.at[0]),
        pltpu.make_async_copy(second_hbm.at[place], second_ref, copied.at[1]),
        pltpu.make_async_copy(gate_hbm, gate_ref, copied.at[2]),
    ]
    for copy in copies:
        copy.start()

    def lay_out(b):
        kv = x_ref[b * shards : (b + 1) * shards, :rows].reshape(part, LANES)
        vk = half_turn(kv)
        keys_ref[here(b), :] = jnp.where(left, kv, vk)
        values_ref[here(b), :] = jnp.where(left, vk, jnp.where(lane == dim, 1.0, 0.0).astype(bf16))

    def queries(b):
        pieces = []
        for i in range(shards):
            x = x_ref[b * shards + i, rows:]
            turned = half_turn(x)
            pieces += [jnp.where(left_q, x, turned), jnp.where(left_q, turned, x)]
        return jnp.concatenate(pieces, axis=0)

    def scores(b):
        scaled = queries(b).astype(f32) * (LOG2E * dim**-0.5)
        high = scaled.astype(bf16)
        low = (scaled - high.astype(f32)).astype(bf16)
        return dot(jnp.where(left, high, low), keys_ref[...], NT)

    def attend(b, score):
        expon = jnp.exp2(score - jnp.max(score, axis=1, keepdims=True)).astype(bf16)
        attended = dot(expon, values_ref[...], NN)
        attended_ref[here(b), :] = attended[:, :dim] * (1.0 / attended[:, dim : dim + 1])

    for b in range(batches):
        lay_out(b)
    score = None if totals_only else scores(0)
    for copy in copies:
        copy.wait()
    first, second = (first_ref[...], second_ref[...])
    first_pair = jnp.concatenate(split(first), axis=0)
    second_centred = split(centred(second))
    second_high, second_low = split(second)
    second_triple = jnp.concatenate([second_high, second_low, second_high], axis=0)

    def hidden(b):
        h, slope = gelu_and_slope(dot(keys_ref[here(b), :], first_pair, NN))
        high_ref[here(b), :], low_ref[here(b), :] = split(h)
        slope_ref[here(b), :] = slope

    def error(b):
        u = project((high_ref[here(b), :], low_ref[here(b), :]), second_centred)
        r = norm_scale(u)
        n = u * r
        e = n - (values_ref[here(b), :dim].astype(f32) - keys_ref[here(b), :dim].astype(f32))
        du = (r * (1.0 / part)) * (
            e - jnp.mean(e, axis=1, keepdims=True) - n * jnp.mean(e * n, axis=1, keepdims=True)
        )
        du_high, du_low = split(du)
        du_ref[here(b), :] = jnp.concatenate([du_high, du_high, du_low], axis=1)

    def add_gradient(b, sums):
        du = du_ref[here(b), :]
        du_high, du_low = (du[:, :dim], du[:, 2 * dim :])
        h_high, h_low = (high_ref[here(b), :], low_ref[here(b), :])
        grad_second = dot(du_high, h_high, TN) + dot(du_low, h_high, TN) + dot(du_high, h_low, TN)
        dz_high, dz_low = split(dot(du, second_triple, NN) * slope_ref[here(b), :])
        k = keys_ref[here(b), :dim]
        sums = (sums[0] + (dot(k, dz_high, TN) + dot(k, dz_low, TN)), sums[1] + grad_second)
        sum_first_ref[b], sum_second_ref[b] = sums
        return sums

    sums = (jnp.zeros((dim, inner), f32), jnp.zeros((dim, inner), f32))
    for step in range(batches + 2):
        if step < batches:
            hidden(step)
        if step + 1 < batches and not totals_only:
            next_score = scores(step + 1)
        if 1 <= step < batches + 1:
            error(step - 1)
        if step < batches and not totals_only:
            attend(step, score)
            score = next_score
        if step >= 2:
            sums = add_gradient(step - 2, sums)
    if totals_only:
        out_ref[0], out_ref[1] = sums
        return

    starts = [[first, second], [first - inner_rate * sums[0], second - inner_rate * sums[1]]]
    if across:
        for way, other in enumerate((before_ref, after_ref)):
            for i in range(2):
                starts[way][i] = starts[way][i] - inner_rate * other[i]
    gates = gate_ref[:, :dim]
    for other in range(1, gate_ref.shape[1] // dim):
        gates = jnp.where(place == other, gate_ref[:, other * dim : (other + 1) * dim], gates)
    gates = jnp.tanh(gates)

    def enter_model(b, way):
        w, v = starts[way]
        if way == 0:
            w, v = (w - inner_rate * sum_first_ref[b], v - inner_rate * sum_second_ref[b])
        elif b > 0:
            w, v = (w + inner_rate * sum_first_ref[b - 1], v + inner_rate * sum_second_ref[b - 1])
        z = dot(queries(b), jnp.concatenate(split(w), axis=0), NN)
        return split(gelu(z)), split(centred(v))

    def leave_model(way, entered):
        u = project(*entered)
        return gates[way : way + 1] * (u * norm_scale(u))

    ahead, behind = (enter_model(0, 0), enter_model(0, 1))
    for b in range(batches):
        last = b + 1 == batches
        next_ahead = None if last else enter_model(b + 1, 0)
        result = leave_model(0, ahead)
        next_behind = None if last else enter_model(b + 1, 1)
        result = result + leave_model(1, behind)
        q = queries(b)[:, :dim].astype(f32)
        result = encode(attended_ref[here(b), :] + (gates[0:1] + gates[1:2]) * q + result)
        out_ref[b] = jnp.concatenate([result[: part // 2], result[part // 2 :]], axis=1)
        ahead, behind = (next_ahead, next_behind)


def work_on_head(x, w_first, w_second, gate_pairs, others=(), totals_only=False):
    dim, inner = w_first.shape[1:]
    tokens = x.shape[0] * (x.shape[1] * 2 // 3)
    if totals_only:
        out = pltpu.VMEM((2, dim, inner), f32)
    else:
        out = pltpu.VMEM((GROUP, tokens // GROUP // 2, LANES), bf16)
    return pl.pallas_call(
        functools.partial(head_kernel, totals_only=totals_only, across=len(others) > 0),
        in_specs=[in_vmem] + [in_hbm] * 3 + [in_vmem] * len(others),
        out_specs=in_vmem,
        scratch_shapes=[
            pltpu.VMEM((dim, inner), f32),
            pltpu.VMEM((dim, inner), f32),
            pltpu.VMEM(gate_pairs.shape, f32),
            pltpu.SemaphoreType.DMA((3,)),
            pltpu.VMEM((tokens, LANES), bf16),
            pltpu.VMEM((tokens, LANES), bf16),
            pltpu.VMEM((tokens, inner), bf16),
            pltpu.VMEM((tokens, inner), bf16),
            pltpu.VMEM((tokens, inner), f32),
            pltpu.VMEM((tokens, 3 * dim), bf16),
            pltpu.VMEM((tokens, dim), f32),
            pltpu.VMEM((GROUP, dim, inner), f32),
            pltpu.VMEM((GROUP, dim, inner), f32),
        ],
        out_shape=out,
        compiler_params=pltpu.CompilerParams(vmem_limit_bytes=52 * 2**20),
        name="totals" if totals_only else "head",
    )(vmem(x), hbm(w_first), hbm(w_second), hbm(gate_pairs), *[vmem(other) for other in others])


def unpack_kernel(packed_ref, out_ref):
    half = packed_ref.shape[1]
    left = left_half(half)
    for pair in range(out_ref.shape[1] // LANES):
        even = packed_ref[2 * pair]
        odd = packed_ref[2 * pair + 1]
        cols = slice(pair * LANES, (pair + 1) * LANES)
        out_ref[:half, cols] = decode(jnp.where(left, even, half_turn(odd)))
        out_ref[half:, cols] = decode(jnp.where(left, half_turn(even), odd))


def unpack(packed, heads_here):
    return pl.pallas_call(
        unpack_kernel,
        in_specs=[in_vmem],
        out_shape=jax.ShapeDtypeStruct((2 * packed.shape[1], heads_here * HEAD_DIM), f32),
        name="unpack",
    )(vmem(packed))


def on_device(queries, key_rows, value_rows, w_first, w_second, gate_pairs):
    seg, sides = (lax.axis_size("seg"), lax.axis_size("head"))
    heads_here = w_first.shape[0]
    segments = seg // GROUP
    assert heads_here <= GROUP
    both = [[s * GROUP * sides + i for i in range(GROUP * sides)] for s in range(segments)]
    lines = [[s * GROUP + i for i in range(GROUP)] for s in range(segments)]
    w_second = jnp.swapaxes(w_second, 1, 2)
    x = pack(queries, key_rows, value_rows, heads_here, sides)
    x = lax.all_to_all(x, ("seg", "head"), 0, 0, tiled=True, axis_index_groups=both)
    others = ()
    if segments > 1:
        totals = work_on_head(x, w_first, w_second, gate_pairs, totals_only=True)
        across = [[s * GROUP + i for s in range(segments)] for i in range(GROUP)]
        here = lax.axis_index("seg") // GROUP
        totals = lax.all_gather(totals, "seg", axis_index_groups=across)
        order = jnp.arange(segments).reshape(-1, 1, 1, 1)
        before = jnp.sum(jnp.where(order < here, totals, 0.0), axis=0)
        after = jnp.sum(jnp.where(order > here, totals, 0.0), axis=0)
        others = (before, after)
    out = work_on_head(x, w_first, w_second, gate_pairs, others)
    out = lax.all_to_all(out, "seg", 0, 0, tiled=True, axis_index_groups=lines)
    return unpack(out, heads_here)


def solution(mesh):
    in_specs = (
        P(("seg", "head"), None),
        P(("seg", "head"), None),
        P(("seg", "head"), None),
        P("head", None, None),
        P("head", None, None),
        P(None, "head"),
    )
    return jax.shard_map(
        on_device, mesh=mesh, in_specs=in_specs, out_specs=P("seg", "head"), check_vma=False
    )
```

```python
import functools

import jax
import jax.numpy as jnp
from jax import lax
from jax.experimental import pallas as pl
from jax.experimental.pallas import tpu as pltpu
from jax.sharding import PartitionSpec as P

HEAD_DIM = 64
GROUP = 8
LANES = 2 * HEAD_DIM

inner_rate = 0.05
norm_epsilon = 1e-05
LOG2E = 1.4426950408889634
BOUND = 36.0
SPREAD = 240.0
GELU_A = 0.7978845608028654
GELU_B = 0.044715

f32, bf16 = (jnp.float32, jnp.bfloat16)
NN = (((1,), (0,)), ((), ()))
NT = (((1,), (1,)), ((), ()))
TN = (((0,), (0,)), ((), ()))


in_vmem = pl.BlockSpec(memory_space=pltpu.VMEM)
in_hbm = pl.BlockSpec(memory_space=pltpu.HBM)


def hbm(x):
    return pltpu.with_memory_space_constraint(x, pltpu.HBM)


def vmem(x):
    return pltpu.with_memory_space_constraint(x, pltpu.VMEM)


def dot(a, b, dims):
    return lax.dot_general(a, b, dims, preferred_element_type=f32)


def split(x):
    high = x.astype(bf16)
    return high, (x - high.astype(f32)).astype(bf16)


def half_turn(x):
    return jnp.concatenate([x[:, HEAD_DIM:], x[:, :HEAD_DIM]], axis=1)


def left_half(rows):
    return lax.broadcasted_iota(jnp.int32, (rows, LANES), 1) < HEAD_DIM


def gelu(z):
    t = jnp.tanh(z * (GELU_A + (GELU_A * GELU_B) * (z * z)))
    half = 0.5 * z
    return half + half * t


def gelu_and_slope(z):
    z2 = z * z
    t = jnp.tanh(z * (GELU_A + (GELU_A * GELU_B) * z2))
    a = 0.5 + 0.5 * t
    return z * a, a + z * (2 * GELU_A + (6 * GELU_A * GELU_B) * z2) * (a * (1 - a))


def centred(second):
    return second - jnp.mean(second, axis=0, keepdims=True)


def project(hidden, second):
    high, low = hidden
    second_high, second_low = second
    return dot(high, second_high, NT) + dot(high, second_low, NT) + dot(low, second_high, NT)


def norm_scale(u):
    return lax.rsqrt(jnp.mean(u * u, axis=1, keepdims=True) + norm_epsilon)


def pack_kernel(q_ref, k_ref, v_ref, out_ref, *, heads_here, sides):
    rows, width = q_ref.shape
    left = left_half(rows)
    left_q = left_half(rows // 2)
    for pair in range(width // LANES):
        cols = slice(pair * LANES, (pair + 1) * LANES)
        k, v, q = (k_ref[:, cols], v_ref[:, cols], q_ref[:, cols])
        k_turned, v_turned = (half_turn(k), half_turn(v))
        qa, qb = (q[: rows // 2], q[rows // 2 :])
        qa_turned, qb_turned = (half_turn(qa), half_turn(qb))
        for odd in range(2):
            head = 2 * pair + odd
            place = (head % heads_here) * sides + head // heads_here
            if odd:
                out_ref[place, :rows] = jnp.where(left, k_turned, v)
                out_ref[place, rows:] = jnp.where(left_q, qa_turned, qb)
            else:
                out_ref[place, :rows] = jnp.where(left, k, v_turned)
                out_ref[place, rows:] = jnp.where(left_q, qa, qb_turned)
    for place in range(heads_here * sides, out_ref.shape[0]):
        out_ref[place] = jnp.zeros(out_ref.shape[1:], bf16)


def pack(queries, key_rows, value_rows, heads_here, sides):
    rows = queries.shape[0]
    return pl.pallas_call(
        functools.partial(pack_kernel, heads_here=heads_here, sides=sides),
        out_specs=in_vmem,
        out_shape=pltpu.VMEM((GROUP * sides, rows + rows // 2, LANES), bf16),
        name="pack",
    )(queries, key_rows, value_rows)


def encode(x):
    y = jnp.exp2(SPREAD * jnp.sqrt(jnp.abs(x) * (1.0 / BOUND)) - SPREAD / 2)
    return jnp.where(x < 0, -y, y).astype(bf16)


def decode(y):
    y = y.astype(f32)
    root = jnp.log2(jnp.abs(y)) * (1.0 / SPREAD) + 0.5
    x = BOUND * (root * root)
    return jnp.where(y < 0, -x, x)


def head_kernel(x_ref, first_hbm, second_hbm, gate_hbm, *rest, totals_only, across):
    if across:
        before_ref, after_ref, *rest = rest
    out_ref, first_ref, second_ref, gate_ref, copied, *rest = rest
    keys_ref, values_ref, high_ref, low_ref, slope_ref, du_ref, attended_ref, sum_first_ref, sum_second_ref = rest
    batches = GROUP
    dim, inner = first_ref.shape
    place = jnp.minimum(lax.axis_index("seg") % GROUP, first_hbm.shape[0] - 1)
    shards = x_ref.shape[0] // batches
    rows = x_ref.shape[1] * 2 // 3
    part = shards * rows
    lane = lax.broadcasted_iota(jnp.int32, (part, LANES), 1)
    left = lane < dim
    left_q = left_half(rows // 2)

    def here(b):
        return slice(b * part, (b + 1) * part)

    copies = [
        pltpu.make_async_copy(first_hbm.at[place], first_ref, copied.at[0]),
        pltpu.make_async_copy(second_hbm.at[place], second_ref, copied.at[1]),
        pltpu.make_async_copy(gate_hbm, gate_ref, copied.at[2]),
    ]
    for copy in copies:
        copy.start()

    def lay_out(b):
        kv = x_ref[b * shards : (b + 1) * shards, :rows].reshape(part, LANES)
        vk = half_turn(kv)
        keys_ref[here(b), :] = jnp.where(left, kv, vk)
        values_ref[here(b), :] = jnp.where(left, vk, jnp.where(lane == dim, 1.0, 0.0).astype(bf16))

    def queries(b):
        pieces = []
        for i in range(shards):
            x = x_ref[b * shards + i, rows:]
            turned = half_turn(x)
            pieces += [jnp.where(left_q, x, turned), jnp.where(left_q, turned, x)]
        return jnp.concatenate(pieces, axis=0)

    def scores(b):
        scaled = queries(b).astype(f32) * (LOG2E * dim**-0.5)
        high = scaled.astype(bf16)
        low = (scaled - high.astype(f32)).astype(bf16)
        return dot(jnp.where(left, high, low), keys_ref[...], NT)

    def attend(b, score):
        expon = jnp.exp2(score - jnp.max(score, axis=1, keepdims=True)).astype(bf16)
        attended = dot(expon, values_ref[...], NN)
        attended_ref[here(b), :] = attended[:, :dim] * (1.0 / attended[:, dim : dim + 1])

    for b in range(batches):
        lay_out(b)
    score = None if totals_only else scores(0)
    for copy in copies:
        copy.wait()
    gates = gate_ref[:, :dim]
    for other in range(1, gate_ref.shape[1] // dim):
        gates = jnp.where(place == other, gate_ref[:, other * dim : (other + 1) * dim], gates)
    gate_ref[:, :dim] = jnp.tanh(gates)
    first, second = (first_ref[...], second_ref[...])
    first_pair = jnp.concatenate(split(first), axis=0)
    second_centred = split(centred(second))
    second_high, second_low = split(second)
    second_triple = jnp.concatenate([second_high, second_low, second_high], axis=0)

    def hidden(b):
        h, slope = gelu_and_slope(dot(keys_ref[here(b), :], first_pair, NN))
        high_ref[here(b), :], low_ref[here(b), :] = split(h)
        slope_ref[here(b), :] = slope

    def error(b):
        u = project((high_ref[here(b), :], low_ref[here(b), :]), second_centred)
        r = norm_scale(u)
        n = u * r
        e = n - (values_ref[here(b), :dim].astype(f32) - keys_ref[here(b), :dim].astype(f32))
        du = (r * (1.0 / part)) * (
            e - jnp.mean(e, axis=1, keepdims=True) - n * jnp.mean(e * n, axis=1, keepdims=True)
        )
        du_high, du_low = split(du)
        du_ref[here(b), :] = jnp.concatenate([du_high, du_high, du_low], axis=1)

    def add_gradient(b, sums):
        du = du_ref[here(b), :]
        du_high, du_low = (du[:, :dim], du[:, 2 * dim :])
        h_high, h_low = (high_ref[here(b), :], low_ref[here(b), :])
        grad_second = dot(du_high, h_high, TN) + dot(du_low, h_high, TN) + dot(du_high, h_low, TN)
        dz_high, dz_low = split(dot(du, second_triple, NN) * slope_ref[here(b), :])
        k = keys_ref[here(b), :dim]
        sums = (sums[0] + (dot(k, dz_high, TN) + dot(k, dz_low, TN)), sums[1] + grad_second)
        sum_first_ref[b], sum_second_ref[b] = sums
        return sums

    sums = (jnp.zeros((dim, inner), f32), jnp.zeros((dim, inner), f32))
    for step in range(batches + 2):
        if step < batches:
            hidden(step)
        if step + 1 < batches and not totals_only:
            next_score = scores(step + 1)
        if 1 <= step < batches + 1:
            error(step - 1)
        if step < batches and not totals_only:
            attend(step, score)
            score = next_score
        if step >= 2:
            sums = add_gradient(step - 2, sums)
    if totals_only:
        out_ref[0], out_ref[1] = sums
        return

    starts = [[first, second], [first - inner_rate * sums[0], second - inner_rate * sums[1]]]
    if across:
        for way, other in enumerate((before_ref, after_ref)):
            for i in range(2):
                starts[way][i] = starts[way][i] - inner_rate * other[i]
    gates = gate_ref[:, :dim]

    def enter_model(b, way):
        w, v = starts[way]
        if way == 0:
            w, v = (w - inner_rate * sum_first_ref[b], v - inner_rate * sum_second_ref[b])
        elif b > 0:
            w, v = (w + inner_rate * sum_first_ref[b - 1], v + inner_rate * sum_second_ref[b - 1])
        z = dot(queries(b), jnp.concatenate(split(w), axis=0), NN)
        return split(gelu(z)), split(centred(v))

    def leave_model(way, entered):
        u = project(*entered)
        return gates[way : way + 1] * (u * norm_scale(u))

    ahead, behind = (enter_model(0, 0), enter_model(0, 1))
    for b in range(batches):
        last = b + 1 == batches
        next_ahead = None if last else enter_model(b + 1, 0)
        result = leave_model(0, ahead)
        next_behind = None if last else enter_model(b + 1, 1)
        result = result + leave_model(1, behind)
        q = queries(b)[:, :dim].astype(f32)
        result = encode(attended_ref[here(b), :] + (gates[0:1] + gates[1:2]) * q + result)
        out_ref[b] = jnp.concatenate([result[: part // 2], result[part // 2 :]], axis=1)
        ahead, behind = (next_ahead, next_behind)


def work_on_head(x, w_first, w_second, gate_pairs, others=(), totals_only=False):
    dim, inner = w_first.shape[1:]
    tokens = x.shape[0] * (x.shape[1] * 2 // 3)
    if totals_only:
        out = pltpu.VMEM((2, dim, inner), f32)
    else:
        out = pltpu.VMEM((GROUP, tokens // GROUP // 2, LANES), bf16)
    return pl.pallas_call(
        functools.partial(head_kernel, totals_only=totals_only, across=len(others) > 0),
        in_specs=[in_vmem] + [in_hbm] * 3 + [in_vmem] * len(others),
        out_specs=in_vmem,
        scratch_shapes=[
            pltpu.VMEM((dim, inner), f32),
            pltpu.VMEM((dim, inner), f32),
            pltpu.VMEM(gate_pairs.shape, f32),
            pltpu.SemaphoreType.DMA((3,)),
            pltpu.VMEM((tokens, LANES), bf16),
            pltpu.VMEM((tokens, LANES), bf16),
            pltpu.VMEM((tokens, inner), bf16),
            pltpu.VMEM((tokens, inner), bf16),
            pltpu.VMEM((tokens, inner), f32),
            pltpu.VMEM((tokens, 3 * dim), bf16),
            pltpu.VMEM((tokens, dim), f32),
            pltpu.VMEM((GROUP, dim, inner), f32),
            pltpu.VMEM((GROUP, dim, inner), f32),
        ],
        out_shape=out,
        compiler_params=pltpu.CompilerParams(vmem_limit_bytes=52 * 2**20),
        name="totals" if totals_only else "head",
    )(vmem(x), hbm(w_first), hbm(w_second), hbm(gate_pairs), *[vmem(other) for other in others])


def unpack_kernel(packed_ref, out_ref):
    half = packed_ref.shape[1]
    left = left_half(half)
    for pair in range(out_ref.shape[1] // LANES):
        even = packed_ref[2 * pair]
        odd = packed_ref[2 * pair + 1]
        cols = slice(pair * LANES, (pair + 1) * LANES)
        out_ref[:half, cols] = decode(jnp.where(left, even, half_turn(odd)))
        out_ref[half:, cols] = decode(jnp.where(left, half_turn(even), odd))


def unpack(packed, heads_here):
    return pl.pallas_call(
        unpack_kernel,
        in_specs=[in_vmem],
        out_shape=jax.ShapeDtypeStruct((2 * packed.shape[1], heads_here * HEAD_DIM), f32),
        name="unpack",
    )(vmem(packed))


def on_device(queries, key_rows, value_rows, w_first, w_second, gate_pairs):
    seg, sides = (lax.axis_size("seg"), lax.axis_size("head"))
    heads_here = w_first.shape[0]
    segments = seg // GROUP
    assert heads_here <= GROUP
    both = [[s * GROUP * sides + i for i in range(GROUP * sides)] for s in range(segments)]
    lines = [[s * GROUP + i for i in range(GROUP)] for s in range(segments)]
    w_second = jnp.swapaxes(w_second, 1, 2)
    x = pack(queries, key_rows, value_rows, heads_here, sides)
    x = lax.all_to_all(x, ("seg", "head"), 0, 0, tiled=True, axis_index_groups=both)
    others = ()
    if segments > 1:
        totals = work_on_head(x, w_first, w_second, gate_pairs, totals_only=True)
        across = [[s * GROUP + i for s in range(segments)] for i in range(GROUP)]
        here = lax.axis_index("seg") // GROUP
        totals = lax.all_gather(totals, "seg", axis_index_groups=across)
        order = jnp.arange(segments).reshape(-1, 1, 1, 1)
        before = jnp.sum(jnp.where(order < here, totals, 0.0), axis=0)
        after = jnp.sum(jnp.where(order > here, totals, 0.0), axis=0)
        others = (before, after)
    out = work_on_head(x, w_first, w_second, gate_pairs, others)
    out = lax.all_to_all(out, "seg", 0, 0, tiled=True, axis_index_groups=lines)
    return unpack(out, heads_here)


def solution(mesh):
    in_specs = (
        P(("seg", "head"), None),
        P(("seg", "head"), None),
        P(("seg", "head"), None),
        P("head", None, None),
        P("head", None, None),
        P(None, "head"),
    )
    return jax.shard_map(
        on_device, mesh=mesh, in_specs=in_specs, out_specs=P("seg", "head"), check_vma=False
    )
```

```python
import functools

import jax
import jax.numpy as jnp
from jax import lax
from jax.experimental import pallas as pl
from jax.experimental.pallas import tpu as pltpu
from jax.sharding import PartitionSpec as P

HEAD_DIM = 64
GROUP = 8
LANES = 2 * HEAD_DIM

inner_rate = 0.05
norm_epsilon = 1e-05
LOG2E = 1.4426950408889634
BOUND = 36.0
SPREAD = 240.0
GELU_A = 0.7978845608028654
GELU_B = 0.044715

f32, bf16 = (jnp.float32, jnp.bfloat16)
NN = (((1,), (0,)), ((), ()))
NT = (((1,), (1,)), ((), ()))
TN = (((0,), (0,)), ((), ()))


in_vmem = pl.BlockSpec(memory_space=pltpu.VMEM)
in_hbm = pl.BlockSpec(memory_space=pltpu.HBM)


def hbm(x):
    return pltpu.with_memory_space_constraint(x, pltpu.HBM)


def vmem(x):
    return pltpu.with_memory_space_constraint(x, pltpu.VMEM)


def dot(a, b, dims):
    return lax.dot_general(a, b, dims, preferred_element_type=f32)


def split(x):
    high = x.astype(bf16)
    return high, (x - high.astype(f32)).astype(bf16)


def half_turn(x):
    return jnp.concatenate([x[:, HEAD_DIM:], x[:, :HEAD_DIM]], axis=1)


def left_half(rows):
    return lax.broadcasted_iota(jnp.int32, (rows, LANES), 1) < HEAD_DIM


def gelu(z):
    t = jnp.tanh(z * (GELU_A + (GELU_A * GELU_B) * (z * z)))
    half = 0.5 * z
    return half + half * t


def gelu_and_slope(z):
    z2 = z * z
    t = jnp.tanh(z * (GELU_A + (GELU_A * GELU_B) * z2))
    a = 0.5 + 0.5 * t
    return z * a, a + z * (2 * GELU_A + (6 * GELU_A * GELU_B) * z2) * (a * (1 - a))


def centred(second):
    return second - jnp.mean(second, axis=0, keepdims=True)


def project(hidden, second):
    high, low = hidden
    second_high, second_low = second
    return dot(high, second_high, NT) + dot(high, second_low, NT) + dot(low, second_high, NT)


def norm_scale(u):
    return lax.rsqrt(jnp.mean(u * u, axis=1, keepdims=True) + norm_epsilon)


def pack_kernel(q_ref, k_ref, v_ref, out_ref, *, heads_here, sides):
    rows, width = q_ref.shape
    left = left_half(rows)
    left_q = left_half(rows // 2)
    for pair in range(width // LANES):
        cols = slice(pair * LANES, (pair + 1) * LANES)
        k, v, q = (k_ref[:, cols], v_ref[:, cols], q_ref[:, cols])
        k_turned, v_turned = (half_turn(k), half_turn(v))
        qa, qb = (q[: rows // 2], q[rows // 2 :])
        qa_turned, qb_turned = (half_turn(qa), half_turn(qb))
        for odd in range(2):
            head = 2 * pair + odd
            place = (head % heads_here) * sides + head // heads_here
            if odd:
                out_ref[place, :rows] = jnp.where(left, k_turned, v)
                out_ref[place, rows:] = jnp.where(left_q, qa_turned, qb)
            else:
                out_ref[place, :rows] = jnp.where(left, k, v_turned)
                out_ref[place, rows:] = jnp.where(left_q, qa, qb_turned)
    for place in range(heads_here * sides, out_ref.shape[0]):
        out_ref[place] = jnp.zeros(out_ref.shape[1:], bf16)


def pack(queries, key_rows, value_rows, heads_here, sides):
    rows = queries.shape[0]
    return pl.pallas_call(
        functools.partial(pack_kernel, heads_here=heads_here, sides=sides),
        out_specs=in_vmem,
        out_shape=pltpu.VMEM((GROUP * sides, rows + rows // 2, LANES), bf16),
        name="pack",
    )(queries, key_rows, value_rows)


def encode(x):
    y = jnp.exp2(SPREAD * jnp.sqrt(jnp.abs(x) * (1.0 / BOUND)) - SPREAD / 2)
    return jnp.where(x < 0, -y, y).astype(bf16)


def decode(y):
    y = y.astype(f32)
    root = jnp.log2(jnp.abs(y)) * (1.0 / SPREAD) + 0.5
    x = BOUND * (root * root)
    return jnp.where(y < 0, -x, x)


def head_kernel(x_ref, first_hbm, second_hbm, gate_hbm, *rest, totals_only, across):
    if across:
        before_ref, after_ref, *rest = rest
    out_ref, first_ref, second_ref, gate_ref, copied, *rest = rest
    keys_ref, values_ref, high_ref, low_ref, slope_ref, du_ref, attended_ref, sum_first_ref, sum_second_ref = rest
    batches = GROUP
    dim, inner = first_ref.shape
    place = jnp.minimum(lax.axis_index("seg") % GROUP, first_hbm.shape[0] - 1)
    shards = x_ref.shape[0] // batches
    rows = x_ref.shape[1] * 2 // 3
    part = shards * rows
    lane = lax.broadcasted_iota(jnp.int32, (part, LANES), 1)
    left = lane < dim
    left_q = left_half(rows // 2)

    def here(b):
        return slice(b * part, (b + 1) * part)

    copies = [
        pltpu.make_async_copy(first_hbm.at[place], first_ref, copied.at[0]),
        pltpu.make_async_copy(second_hbm.at[place], second_ref, copied.at[1]),
        pltpu.make_async_copy(gate_hbm, gate_ref, copied.at[2]),
    ]
    for copy in copies:
        copy.start()

    def lay_out(b):
        kv = x_ref[b * shards : (b + 1) * shards, :rows].reshape(part, LANES)
        vk = half_turn(kv)
        keys_ref[here(b), :] = jnp.where(left, kv, vk)
        values_ref[here(b), :] = jnp.where(left, vk, jnp.where(lane == dim, 1.0, 0.0).astype(bf16))

    def queries(b):
        pieces = []
        for i in range(shards):
            x = x_ref[b * shards + i, rows:]
            turned = half_turn(x)
            pieces += [jnp.where(left_q, x, turned), jnp.where(left_q, turned, x)]
        return jnp.concatenate(pieces, axis=0)

    def scores(b):
        scaled = queries(b).astype(f32) * (LOG2E * dim**-0.5)
        high = scaled.astype(bf16)
        low = (scaled - high.astype(f32)).astype(bf16)
        return dot(jnp.where(left, high, low), keys_ref[...], NT)

    def attend(b, score):
        expon = jnp.exp2(score - jnp.max(score, axis=1, keepdims=True)).astype(bf16)
        attended = dot(expon, values_ref[...], NN)
        attended_ref[here(b), :] = attended[:, :dim] * (1.0 / attended[:, dim : dim + 1])

    for b in range(batches):
        lay_out(b)
    score = None if totals_only else scores(0)
    for copy in copies:
        copy.wait()
    gates = gate_ref[:, :dim]
    for other in range(1, gate_ref.shape[1] // dim):
        gates = jnp.where(place == other, gate_ref[:, other * dim : (other + 1) * dim], gates)
    gate_ref[:, :dim] = jnp.tanh(gates)
    first, second = (first_ref[...], second_ref[...])
    first_pair = jnp.concatenate(split(first), axis=0)
    second_centred = split(centred(second))
    second_high, second_low = split(second)
    second_triple = jnp.concatenate([second_high, second_high, second_low], axis=0)

    def hidden(b):
        h, slope = gelu_and_slope(dot(keys_ref[here(b), :], first_pair, NN))
        high_ref[here(b), :], low_ref[here(b), :] = split(h)
        slope_ref[here(b), :] = slope

    def error(b):
        u = project((high_ref[here(b), :], low_ref[here(b), :]), second_centred)
        r = norm_scale(u)
        n = u * r
        e = n - (values_ref[here(b), :dim].astype(f32) - keys_ref[here(b), :dim].astype(f32))
        du = (r * (1.0 / part)) * (
            e - jnp.mean(e, axis=1, keepdims=True) - n * jnp.mean(e * n, axis=1, keepdims=True)
        )
        du_high, du_low = split(du)
        du_ref[here(b), :] = jnp.concatenate([du_high, du_low, du_high], axis=1)

    def add_gradient(b, sums):
        du = du_ref[here(b), :]
        du_high = du[:, :dim]
        h_high, h_low = (high_ref[here(b), :], low_ref[here(b), :])
        both = dot(du[:, : 2 * dim], h_high, TN)
        grad_second = both[:dim] + both[dim:] + dot(du_high, h_low, TN)
        dz_high, dz_low = split(dot(du, second_triple, NN) * slope_ref[here(b), :])
        k = keys_ref[here(b), :dim]
        sums = (sums[0] + (dot(k, dz_high, TN) + dot(k, dz_low, TN)), sums[1] + grad_second)
        sum_first_ref[b], sum_second_ref[b] = sums
        return sums

    sums = (jnp.zeros((dim, inner), f32), jnp.zeros((dim, inner), f32))
    for step in range(batches + 2):
        if step < batches:
            hidden(step)
        if step + 1 < batches and not totals_only:
            next_score = scores(step + 1)
        if 1 <= step < batches + 1:
            error(step - 1)
        if step < batches and not totals_only:
            attend(step, score)
            score = next_score
        if step >= 2:
            sums = add_gradient(step - 2, sums)
    if totals_only:
        out_ref[0], out_ref[1] = sums
        return

    starts = [[first, second], [first - inner_rate * sums[0], second - inner_rate * sums[1]]]
    if across:
        for way, other in enumerate((before_ref, after_ref)):
            for i in range(2):
                starts[way][i] = starts[way][i] - inner_rate * other[i]
    gates = gate_ref[:, :dim]

    def enter_model(b, way):
        w, v = starts[way]
        if way == 0:
            w, v = (w - inner_rate * sum_first_ref[b], v - inner_rate * sum_second_ref[b])
        elif b > 0:
            w, v = (w + inner_rate * sum_first_ref[b - 1], v + inner_rate * sum_second_ref[b - 1])
        z = dot(queries(b), jnp.concatenate(split(w), axis=0), NN)
        return split(gelu(z)), split(centred(v))

    def leave_model(way, entered):
        u = project(*entered)
        return gates[way : way + 1] * (u * norm_scale(u))

    ahead, behind = (enter_model(0, 0), enter_model(0, 1))
    for b in range(batches):
        last = b + 1 == batches
        next_ahead = None if last else enter_model(b + 1, 0)
        result = leave_model(0, ahead)
        next_behind = None if last else enter_model(b + 1, 1)
        result = result + leave_model(1, behind)
        q = queries(b)[:, :dim].astype(f32)
        result = encode(attended_ref[here(b), :] + (gates[0:1] + gates[1:2]) * q + result)
        out_ref[b] = jnp.concatenate([result[: part // 2], result[part // 2 :]], axis=1)
        ahead, behind = (next_ahead, next_behind)


def work_on_head(x, w_first, w_second, gate_pairs, others=(), totals_only=False):
    dim, inner = w_first.shape[1:]
    tokens = x.shape[0] * (x.shape[1] * 2 // 3)
    if totals_only:
        out = pltpu.VMEM((2, dim, inner), f32)
    else:
        out = pltpu.VMEM((GROUP, tokens // GROUP // 2, LANES), bf16)
    return pl.pallas_call(
        functools.partial(head_kernel, totals_only=totals_only, across=len(others) > 0),
        in_specs=[in_vmem] + [in_hbm] * 3 + [in_vmem] * len(others),
        out_specs=in_vmem,
        scratch_shapes=[
            pltpu.VMEM((dim, inner), f32),
            pltpu.VMEM((dim, inner), f32),
            pltpu.VMEM(gate_pairs.shape, f32),
            pltpu.SemaphoreType.DMA((3,)),
            pltpu.VMEM((tokens, LANES), bf16),
            pltpu.VMEM((tokens, LANES), bf16),
            pltpu.VMEM((tokens, inner), bf16),
            pltpu.VMEM((tokens, inner), bf16),
            pltpu.VMEM((tokens, inner), f32),
            pltpu.VMEM((tokens, 3 * dim), bf16),
            pltpu.VMEM((tokens, dim), f32),
            pltpu.VMEM((GROUP, dim, inner), f32),
            pltpu.VMEM((GROUP, dim, inner), f32),
        ],
        out_shape=out,
        compiler_params=pltpu.CompilerParams(vmem_limit_bytes=52 * 2**20),
        name="totals" if totals_only else "head",
    )(vmem(x), hbm(w_first), hbm(w_second), hbm(gate_pairs), *[vmem(other) for other in others])


def unpack_kernel(packed_ref, out_ref):
    half = packed_ref.shape[1]
    left = left_half(half)
    for pair in range(out_ref.shape[1] // LANES):
        even = packed_ref[2 * pair]
        odd = packed_ref[2 * pair + 1]
        cols = slice(pair * LANES, (pair + 1) * LANES)
        out_ref[:half, cols] = decode(jnp.where(left, even, half_turn(odd)))
        out_ref[half:, cols] = decode(jnp.where(left, half_turn(even), odd))


def unpack(packed, heads_here):
    return pl.pallas_call(
        unpack_kernel,
        in_specs=[in_vmem],
        out_shape=jax.ShapeDtypeStruct((2 * packed.shape[1], heads_here * HEAD_DIM), f32),
        name="unpack",
    )(vmem(packed))


def on_device(queries, key_rows, value_rows, w_first, w_second, gate_pairs):
    seg, sides = (lax.axis_size("seg"), lax.axis_size("head"))
    heads_here = w_first.shape[0]
    segments = seg // GROUP
    assert heads_here <= GROUP
    both = [[s * GROUP * sides + i for i in range(GROUP * sides)] for s in range(segments)]
    lines = [[s * GROUP + i for i in range(GROUP)] for s in range(segments)]
    w_second = jnp.swapaxes(w_second, 1, 2)
    x = pack(queries, key_rows, value_rows, heads_here, sides)
    x = lax.all_to_all(x, ("seg", "head"), 0, 0, tiled=True, axis_index_groups=both)
    others = ()
    if segments > 1:
        totals = work_on_head(x, w_first, w_second, gate_pairs, totals_only=True)
        across = [[s * GROUP + i for s in range(segments)] for i in range(GROUP)]
        here = lax.axis_index("seg") // GROUP
        totals = lax.all_gather(totals, "seg", axis_index_groups=across)
        order = jnp.arange(segments).reshape(-1, 1, 1, 1)
        before = jnp.sum(jnp.where(order < here, totals, 0.0), axis=0)
        after = jnp.sum(jnp.where(order > here, totals, 0.0), axis=0)
        others = (before, after)
    out = work_on_head(x, w_first, w_second, gate_pairs, others)
    out = lax.all_to_all(out, "seg", 0, 0, tiled=True, axis_index_groups=lines)
    return unpack(out, heads_here)


def solution(mesh):
    in_specs = (
        P(("seg", "head"), None),
        P(("seg", "head"), None),
        P(("seg", "head"), None),
        P("head", None, None),
        P("head", None, None),
        P(None, "head"),
    )
    return jax.shard_map(
        on_device, mesh=mesh, in_specs=in_specs, out_specs=P("seg", "head"), check_vma=False
    )
```

```python
import functools

import jax
import jax.numpy as jnp
from jax import lax
from jax.experimental import pallas as pl
from jax.experimental.pallas import tpu as pltpu
from jax.sharding import PartitionSpec as P

HEAD_DIM = 64
GROUP = 8
LANES = 2 * HEAD_DIM

inner_rate = 0.05
norm_epsilon = 1e-05
LOG2E = 1.4426950408889634
BOUND = 36.0
SPREAD = 240.0
GELU_A = 0.7978845608028654
GELU_B = 0.044715

f32, bf16 = (jnp.float32, jnp.bfloat16)
NN = (((1,), (0,)), ((), ()))
NT = (((1,), (1,)), ((), ()))
TN = (((0,), (0,)), ((), ()))


in_vmem = pl.BlockSpec(memory_space=pltpu.VMEM)
in_hbm = pl.BlockSpec(memory_space=pltpu.HBM)


def hbm(x):
    return pltpu.with_memory_space_constraint(x, pltpu.HBM)


def vmem(x):
    return pltpu.with_memory_space_constraint(x, pltpu.VMEM)


def dot(a, b, dims):
    return lax.dot_general(a, b, dims, preferred_element_type=f32)


def split(x):
    high = x.astype(bf16)
    return high, (x - high.astype(f32)).astype(bf16)


def half_turn(x):
    return jnp.concatenate([x[:, HEAD_DIM:], x[:, :HEAD_DIM]], axis=1)


def left_half(rows):
    return lax.broadcasted_iota(jnp.int32, (rows, LANES), 1) < HEAD_DIM


def gelu(z):
    t = jnp.tanh(z * (GELU_A + (GELU_A * GELU_B) * (z * z)))
    half = 0.5 * z
    return half + half * t


def gelu_and_slope(z):
    z2 = z * z
    t = jnp.tanh(z * (GELU_A + (GELU_A * GELU_B) * z2))
    a = 0.5 + 0.5 * t
    return z * a, a + z * (2 * GELU_A + (6 * GELU_A * GELU_B) * z2) * (a * (1 - a))


def centred(second):
    return second - jnp.mean(second, axis=0, keepdims=True)


def project(hidden, second):
    high, low = hidden
    second_high, second_low = second
    return dot(high, second_high, NT) + dot(high, second_low, NT) + dot(low, second_high, NT)


def norm_scale(u):
    return lax.rsqrt(jnp.mean(u * u, axis=1, keepdims=True) + norm_epsilon)


def pack_kernel(q_ref, k_ref, v_ref, out_ref, *, heads_here, sides):
    rows, width = q_ref.shape
    left = left_half(rows)
    left_q = left_half(rows // 2)
    for pair in range(width // LANES):
        cols = slice(pair * LANES, (pair + 1) * LANES)
        k, v, q = (k_ref[:, cols], v_ref[:, cols], q_ref[:, cols])
        k_turned, v_turned = (half_turn(k), half_turn(v))
        qa, qb = (q[: rows // 2], q[rows // 2 :])
        qa_turned, qb_turned = (half_turn(qa), half_turn(qb))
        for odd in range(2):
            head = 2 * pair + odd
            place = (head % heads_here) * sides + head // heads_here
            if odd:
                out_ref[place, :rows] = jnp.where(left, k_turned, v)
                out_ref[place, rows:] = jnp.where(left_q, qa_turned, qb)
            else:
                out_ref[place, :rows] = jnp.where(left, k, v_turned)
                out_ref[place, rows:] = jnp.where(left_q, qa, qb_turned)
    for place in range(heads_here * sides, out_ref.shape[0]):
        out_ref[place] = jnp.zeros(out_ref.shape[1:], bf16)


def pack(queries, key_rows, value_rows, heads_here, sides):
    rows = queries.shape[0]
    return pl.pallas_call(
        functools.partial(pack_kernel, heads_here=heads_here, sides=sides),
        out_specs=in_vmem,
        out_shape=pltpu.VMEM((GROUP * sides, rows + rows // 2, LANES), bf16),
        name="pack",
    )(queries, key_rows, value_rows)


def encode(x):
    y = jnp.exp2(SPREAD * jnp.sqrt(jnp.abs(x) * (1.0 / BOUND)) - SPREAD / 2)
    return jnp.where(x < 0, -y, y).astype(bf16)


def decode(y):
    y = y.astype(f32)
    root = jnp.log2(jnp.abs(y)) * (1.0 / SPREAD) + 0.5
    x = BOUND * (root * root)
    return jnp.where(y < 0, -x, x)


def head_kernel(x_ref, first_hbm, second_hbm, gate_hbm, *rest, totals_only, across):
    if across:
        before_ref, after_ref, *rest = rest
    out_ref, first_ref, second_ref, gate_ref, copied, *rest = rest
    keys_ref, values_ref, high_ref, low_ref, slope_ref, du_ref, attended_ref, sum_first_ref, sum_second_ref = rest
    batches = GROUP
    dim, inner = first_ref.shape
    place = jnp.minimum(lax.axis_index("seg") % GROUP, first_hbm.shape[0] - 1)
    shards = x_ref.shape[0] // batches
    rows = x_ref.shape[1] * 2 // 3
    part = shards * rows
    lane = lax.broadcasted_iota(jnp.int32, (part, LANES), 1)
    left = lane < dim
    left_q = left_half(rows // 2)

    def here(b):
        return slice(b * part, (b + 1) * part)

    copies = [
        pltpu.make_async_copy(first_hbm.at[place], first_ref, copied.at[0]),
        pltpu.make_async_copy(second_hbm.at[place], second_ref, copied.at[1]),
        pltpu.make_async_copy(gate_hbm, gate_ref, copied.at[2]),
    ]
    for copy in copies:
        copy.start()

    def lay_out(b):
        kv = x_ref[b * shards : (b + 1) * shards, :rows].reshape(part, LANES)
        vk = half_turn(kv)
        keys_ref[here(b), :] = jnp.where(left, kv, vk)
        values_ref[here(b), :] = jnp.where(left, vk, jnp.where(lane == dim, 1.0, 0.0).astype(bf16))

    def queries(b):
        pieces = []
        for i in range(shards):
            x = x_ref[b * shards + i, rows:]
            turned = half_turn(x)
            pieces += [jnp.where(left_q, x, turned), jnp.where(left_q, turned, x)]
        return jnp.concatenate(pieces, axis=0)

    def scores(b):
        scaled = queries(b).astype(f32) * (LOG2E * dim**-0.5)
        high = scaled.astype(bf16)
        low = (scaled - high.astype(f32)).astype(bf16)
        return dot(jnp.where(left, high, low), keys_ref[...], NT)

    def attend(b, score):
        expon = jnp.exp2(score - jnp.max(score, axis=1, keepdims=True)).astype(bf16)
        attended = dot(expon, values_ref[...], NN)
        attended_ref[here(b), :] = attended[:, :dim] * (1.0 / attended[:, dim : dim + 1])

    for b in range(batches):
        lay_out(b)
    score = None if totals_only else scores(0)
    for copy in copies:
        copy.wait()
    gates = gate_ref[:, :dim]
    for other in range(1, gate_ref.shape[1] // dim):
        gates = jnp.where(place == other, gate_ref[:, other * dim : (other + 1) * dim], gates)
    gate_ref[:, :dim] = jnp.tanh(gates)
    first, second = (first_ref[...], second_ref[...])
    first_pair = jnp.concatenate(split(first), axis=0)
    second_centred = split(centred(second))
    second_high, second_low = split(second)
    second_triple = jnp.concatenate([second_high, second_high, second_low], axis=0)

    def hidden(b):
        h, slope = gelu_and_slope(dot(keys_ref[here(b), :], first_pair, NN))
        high_ref[here(b), :], low_ref[here(b), :] = split(h)
        slope_ref[here(b), :] = slope

    def error(b):
        u = project((high_ref[here(b), :], low_ref[here(b), :]), second_centred)
        r = norm_scale(u)
        n = u * r
        e = n - (values_ref[here(b), :dim].astype(f32) - keys_ref[here(b), :dim].astype(f32))
        du = (r * (1.0 / part)) * (
            e - jnp.mean(e, axis=1, keepdims=True) - n * jnp.mean(e * n, axis=1, keepdims=True)
        )
        du_high, du_low = split(du)
        du_ref[here(b), :] = jnp.concatenate([du_high, du_low, du_high], axis=1)

    def add_gradient(b, sums):
        du = du_ref[here(b), :]
        du_high = du[:, :dim]
        h_high, h_low = (high_ref[here(b), :], low_ref[here(b), :])
        both = dot(du[:, : 2 * dim], h_high, TN)
        grad_second = both[:dim] + both[dim:] + dot(du_high, h_low, TN)
        dz_high, dz_low = split(dot(du, second_triple, NN) * slope_ref[here(b), :])
        k = keys_ref[here(b), :dim]
        sums = (sums[0] + (dot(k, dz_high, TN) + dot(k, dz_low, TN)), sums[1] + grad_second)
        sum_first_ref[b], sum_second_ref[b] = sums
        return sums

    sums = (jnp.zeros((dim, inner), f32), jnp.zeros((dim, inner), f32))
    for step in range(batches + 2):
        if step < batches:
            hidden(step)
        if step + 1 < batches and not totals_only:
            next_score = scores(step + 1)
        if 1 <= step < batches + 1:
            error(step - 1)
        if step < batches and not totals_only:
            attend(step, score)
            score = next_score
        if step >= 2:
            sums = add_gradient(step - 2, sums)
    if totals_only:
        out_ref[0], out_ref[1] = sums
        return

    starts = [[first, second], [first - inner_rate * sums[0], second - inner_rate * sums[1]]]
    if across:
        for way, other in enumerate((before_ref, after_ref)):
            for i in range(2):
                starts[way][i] = starts[way][i] - inner_rate * other[i]
    gates = gate_ref[:, :dim]

    def enter_model(b, way):
        w, v = starts[way]
        if way == 0:
            w, v = (w - inner_rate * sum_first_ref[b], v - inner_rate * sum_second_ref[b])
        elif b > 0:
            w, v = (w + inner_rate * sum_first_ref[b - 1], v + inner_rate * sum_second_ref[b - 1])
        z = dot(queries(b), jnp.concatenate(split(w), axis=0), NN)
        return split(gelu(z)), split(centred(v))

    def leave_model(way, entered):
        u = project(*entered)
        return gates[way : way + 1] * (u * norm_scale(u))

    ahead, behind = (enter_model(0, 0), enter_model(0, 1))
    for b in range(batches):
        last = b + 1 == batches
        next_ahead = None if last else enter_model(b + 1, 0)
        result = leave_model(0, ahead)
        next_behind = None if last else enter_model(b + 1, 1)
        result = result + leave_model(1, behind)
        q = queries(b)[:, :dim].astype(f32)
        result = encode(attended_ref[here(b), :] + (gates[0:1] + gates[1:2]) * q + result)
        out_ref[b] = jnp.concatenate([result[: part // 2], result[part // 2 :]], axis=1)
        ahead, behind = (next_ahead, next_behind)


def work_on_head(x, w_first, w_second, gate_pairs, others=(), totals_only=False):
    dim, inner = w_first.shape[1:]
    tokens = x.shape[0] * (x.shape[1] * 2 // 3)
    if totals_only:
        out = pltpu.VMEM((2, dim, inner), f32)
    else:
        out = pltpu.VMEM((GROUP, tokens // GROUP // 2, LANES), bf16)
    return pl.pallas_call(
        functools.partial(head_kernel, totals_only=totals_only, across=len(others) > 0),
        in_specs=[in_vmem] + [in_hbm] * 3 + [in_vmem] * len(others),
        out_specs=in_vmem,
        scratch_shapes=[
            pltpu.VMEM((dim, inner), f32),
            pltpu.VMEM((dim, inner), f32),
            pltpu.VMEM(gate_pairs.shape, f32),
            pltpu.SemaphoreType.DMA((3,)),
            pltpu.VMEM((tokens, LANES), bf16),
            pltpu.VMEM((tokens, LANES), bf16),
            pltpu.VMEM((tokens, inner), bf16),
            pltpu.VMEM((tokens, inner), bf16),
            pltpu.VMEM((tokens, inner), f32),
            pltpu.VMEM((tokens, 3 * dim), bf16),
            pltpu.VMEM((tokens, dim), f32),
            pltpu.VMEM((GROUP, dim, inner), f32),
            pltpu.VMEM((GROUP, dim, inner), f32),
        ],
        out_shape=out,
        compiler_params=pltpu.CompilerParams(vmem_limit_bytes=52 * 2**20),
        name="totals" if totals_only else "head",
    )(vmem(x), hbm(w_first), hbm(w_second), hbm(gate_pairs), *[vmem(other) for other in others])


def unpack_kernel(packed_ref, out_hbm, rows_ref, copied):
    half = packed_ref.shape[1]
    left = left_half(half)
    copies = []
    for second in range(2):
        here = pl.ds(second * half, half)
        for pair in range(rows_ref.shape[1] // LANES):
            even = packed_ref[2 * pair]
            odd = packed_ref[2 * pair + 1]
            cols = slice(pair * LANES, (pair + 1) * LANES)
            if second:
                rows_ref[here, cols] = decode(jnp.where(left, half_turn(even), odd))
            else:
                rows_ref[here, cols] = decode(jnp.where(left, even, half_turn(odd)))
        copies.append(pltpu.make_async_copy(rows_ref.at[here], out_hbm.at[here], copied.at[second]))
        copies[second].start()
    for copy in copies:
        copy.wait()


def unpack(packed, heads_here):
    out = (2 * packed.shape[1], heads_here * HEAD_DIM)
    return pl.pallas_call(
        unpack_kernel,
        in_specs=[in_vmem],
        out_specs=in_hbm,
        out_shape=jax.ShapeDtypeStruct(out, f32),
        scratch_shapes=[pltpu.VMEM(out, f32), pltpu.SemaphoreType.DMA((2,))],
        name="unpack",
    )(vmem(packed))


def on_device(queries, key_rows, value_rows, w_first, w_second, gate_pairs):
    seg, sides = (lax.axis_size("seg"), lax.axis_size("head"))
    heads_here = w_first.shape[0]
    segments = seg // GROUP
    assert heads_here <= GROUP
    both = [[s * GROUP * sides + i for i in range(GROUP * sides)] for s in range(segments)]
    lines = [[s * GROUP + i for i in range(GROUP)] for s in range(segments)]
    w_second = jnp.swapaxes(w_second, 1, 2)
    x = pack(queries, key_rows, value_rows, heads_here, sides)
    x = lax.all_to_all(x, ("seg", "head"), 0, 0, tiled=True, axis_index_groups=both)
    others = ()
    if segments > 1:
        totals = work_on_head(x, w_first, w_second, gate_pairs, totals_only=True)
        across = [[s * GROUP + i for s in range(segments)] for i in range(GROUP)]
        here = lax.axis_index("seg") // GROUP
        totals = lax.all_gather(totals, "seg", axis_index_groups=across)
        order = jnp.arange(segments).reshape(-1, 1, 1, 1)
        before = jnp.sum(jnp.where(order < here, totals, 0.0), axis=0)
        after = jnp.sum(jnp.where(order > here, totals, 0.0), axis=0)
        others = (before, after)
    out = work_on_head(x, w_first, w_second, gate_pairs, others)
    out = lax.all_to_all(out, "seg", 0, 0, tiled=True, axis_index_groups=lines)
    return unpack(out, heads_here)


def solution(mesh):
    in_specs = (
        P(("seg", "head"), None),
        P(("seg", "head"), None),
        P(("seg", "head"), None),
        P("head", None, None),
        P("head", None, None),
        P(None, "head"),
    )
    return jax.shard_map(
        on_device, mesh=mesh, in_specs=in_specs, out_specs=P("seg", "head"), check_vma=False
    )
```

```python
import functools

import jax
import jax.numpy as jnp
from jax import lax
from jax.experimental import pallas as pl
from jax.experimental.pallas import tpu as pltpu
from jax.sharding import PartitionSpec as P

HEAD_DIM = 64
GROUP = 8
LANES = 2 * HEAD_DIM

inner_rate = 0.05
norm_epsilon = 1e-05
LOG2E = 1.4426950408889634
BOUND = 36.0
SPREAD = 240.0
GELU_A = 0.7978845608028654
GELU_B = 0.044715

f32, bf16 = (jnp.float32, jnp.bfloat16)
NN = (((1,), (0,)), ((), ()))
NT = (((1,), (1,)), ((), ()))
TN = (((0,), (0,)), ((), ()))


in_vmem = pl.BlockSpec(memory_space=pltpu.VMEM)
in_hbm = pl.BlockSpec(memory_space=pltpu.HBM)


def hbm(x):
    return pltpu.with_memory_space_constraint(x, pltpu.HBM)


def vmem(x):
    return pltpu.with_memory_space_constraint(x, pltpu.VMEM)


def dot(a, b, dims):
    return lax.dot_general(a, b, dims, preferred_element_type=f32)


def split(x):
    high = x.astype(bf16)
    return high, (x - high.astype(f32)).astype(bf16)


def half_turn(x):
    return jnp.concatenate([x[:, HEAD_DIM:], x[:, :HEAD_DIM]], axis=1)


def left_half(rows):
    return lax.broadcasted_iota(jnp.int32, (rows, LANES), 1) < HEAD_DIM


def gelu(z):
    t = jnp.tanh(z * (GELU_A + (GELU_A * GELU_B) * (z * z)))
    half = 0.5 * z
    return half + half * t


def gelu_and_slope(z):
    z2 = z * z
    t = jnp.tanh(z * (GELU_A + (GELU_A * GELU_B) * z2))
    a = 0.5 + 0.5 * t
    return z * a, a + z * (2 * GELU_A + (6 * GELU_A * GELU_B) * z2) * (a * (1 - a))


def centred(second):
    return second - jnp.mean(second, axis=0, keepdims=True)


def project(hidden, second):
    high, low = hidden
    second_high, second_low = second
    return dot(high, second_high, NT) + dot(high, second_low, NT) + dot(low, second_high, NT)


def norm_scale(u):
    return lax.rsqrt(jnp.mean(u * u, axis=1, keepdims=True) + norm_epsilon)


def pack_kernel(q_ref, k_ref, v_ref, out_ref, *, heads_here, sides):
    rows, width = q_ref.shape
    left = left_half(rows)
    left_q = left_half(rows // 2)
    for pair in range(width // LANES):
        cols = slice(pair * LANES, (pair + 1) * LANES)
        k, v, q = (k_ref[:, cols], v_ref[:, cols], q_ref[:, cols])
        k_turned, v_turned = (half_turn(k), half_turn(v))
        qa, qb = (q[: rows // 2], q[rows // 2 :])
        qa_turned, qb_turned = (half_turn(qa), half_turn(qb))
        for odd in range(2):
            head = 2 * pair + odd
            place = (head % heads_here) * sides + head // heads_here
            if odd:
                out_ref[place, :rows] = jnp.where(left, k_turned, v)
                out_ref[place, rows:] = jnp.where(left_q, qa_turned, qb)
            else:
                out_ref[place, :rows] = jnp.where(left, k, v_turned)
                out_ref[place, rows:] = jnp.where(left_q, qa, qb_turned)
    for place in range(heads_here * sides, out_ref.shape[0]):
        out_ref[place] = jnp.zeros(out_ref.shape[1:], bf16)


def pack(queries, key_rows, value_rows, heads_here, sides):
    rows = queries.shape[0]
    return pl.pallas_call(
        functools.partial(pack_kernel, heads_here=heads_here, sides=sides),
        out_specs=in_vmem,
        out_shape=pltpu.VMEM((GROUP * sides, rows + rows // 2, LANES), bf16),
        name="pack",
    )(queries, key_rows, value_rows)


def encode(x):
    y = jnp.exp2(SPREAD * jnp.sqrt(jnp.abs(x) * (1.0 / BOUND)) - SPREAD / 2)
    return jnp.where(x < 0, -y, y).astype(bf16)


def decode(y):
    y = y.astype(f32)
    root = jnp.log2(jnp.abs(y)) * (1.0 / SPREAD) + 0.5
    x = BOUND * (root * root)
    return jnp.where(y < 0, -x, x)


def head_kernel(x_ref, first_hbm, second_hbm, gate_hbm, *rest, totals_only, across):
    if across:
        before_ref, after_ref, *rest = rest
    out_ref, first_ref, second_ref, gate_ref, copied, *rest = rest
    keys_ref, values_ref, high_ref, low_ref, slope_ref, du_ref, attended_ref, sum_first_ref, sum_second_ref = rest
    batches = GROUP
    dim, inner = first_ref.shape
    place = jnp.minimum(lax.axis_index("seg") % GROUP, first_hbm.shape[0] - 1)
    shards = x_ref.shape[0] // batches
    rows = x_ref.shape[1] * 2 // 3
    part = shards * rows
    lane = lax.broadcasted_iota(jnp.int32, (part, LANES), 1)
    left = lane < dim
    left_q = left_half(rows // 2)

    def here(b):
        return slice(b * part, (b + 1) * part)

    copies = [
        pltpu.make_async_copy(first_hbm.at[place], first_ref, copied.at[0]),
        pltpu.make_async_copy(second_hbm.at[place], second_ref, copied.at[1]),
        pltpu.make_async_copy(gate_hbm, gate_ref, copied.at[2]),
    ]
    for copy in copies:
        copy.start()

    def lay_out(b):
        kv = x_ref[b * shards : (b + 1) * shards, :rows].reshape(part, LANES)
        vk = half_turn(kv)
        keys_ref[here(b), :] = jnp.where(left, kv, vk)
        values_ref[here(b), :] = jnp.where(left, vk, jnp.where(lane == dim, 1.0, 0.0).astype(bf16))

    def queries(b):
        pieces = []
        for i in range(shards):
            x = x_ref[b * shards + i, rows:]
            turned = half_turn(x)
            pieces += [jnp.where(left_q, x, turned), jnp.where(left_q, turned, x)]
        return jnp.concatenate(pieces, axis=0)

    def scores(b):
        scaled = queries(b).astype(f32) * (LOG2E * dim**-0.5)
        high = scaled.astype(bf16)
        low = (scaled - high.astype(f32)).astype(bf16)
        return dot(jnp.where(left, high, low), keys_ref[...], NT)

    def attend(b, score):
        expon = jnp.exp2(score - jnp.max(score, axis=1, keepdims=True)).astype(bf16)
        attended = dot(expon, values_ref[...], NN)
        attended_ref[here(b), :] = attended[:, :dim] * (1.0 / attended[:, dim : dim + 1])

    for b in range(batches):
        lay_out(b)
    score = None if totals_only else scores(0)
    for copy in copies:
        copy.wait()
    gates = gate_ref[:, :dim]
    for other in range(1, gate_ref.shape[1] // dim):
        gates = jnp.where(place == other, gate_ref[:, other * dim : (other + 1) * dim], gates)
    gate_ref[:, :dim] = jnp.tanh(gates)
    first, second = (first_ref[...], second_ref[...])
    first_pair = jnp.concatenate(split(first), axis=0)
    second_centred = split(centred(second))
    second_high, second_low = split(second)
    second_triple = jnp.concatenate([second_high, second_high, second_low], axis=0)

    def hidden(b):
        h, slope = gelu_and_slope(dot(keys_ref[here(b), :], first_pair, NN))
        high_ref[here(b), :], low_ref[here(b), :] = split(h)
        slope_ref[here(b), :] = slope

    def error(b):
        u = project((high_ref[here(b), :], low_ref[here(b), :]), second_centred)
        r = norm_scale(u)
        n = u * r
        e = n - (values_ref[here(b), :dim].astype(f32) - keys_ref[here(b), :dim].astype(f32))
        du = (r * (1.0 / part)) * (
            e - jnp.mean(e, axis=1, keepdims=True) - n * jnp.mean(e * n, axis=1, keepdims=True)
        )
        du_high, du_low = split(du)
        du_ref[here(b), :] = jnp.concatenate([du_high, du_low, du_high], axis=1)

    def add_gradient(b, sums):
        du = du_ref[here(b), :]
        du_high = du[:, :dim]
        h_high, h_low = (high_ref[here(b), :], low_ref[here(b), :])
        both = dot(du[:, : 2 * dim], h_high, TN)
        grad_second = both[:dim] + both[dim:] + dot(du_high, h_low, TN)
        dz_high, dz_low = split(dot(du, second_triple, NN) * slope_ref[here(b), :])
        k = keys_ref[here(b), :dim]
        sums = (sums[0] + (dot(k, dz_high, TN) + dot(k, dz_low, TN)), sums[1] + grad_second)
        sum_first_ref[b], sum_second_ref[b] = sums
        return sums

    sums = (jnp.zeros((dim, inner), f32), jnp.zeros((dim, inner), f32))
    for step in range(batches + 2):
        if step < batches:
            hidden(step)
        if step + 1 < batches and not totals_only:
            next_score = scores(step + 1)
        if 1 <= step < batches + 1:
            error(step - 1)
        if step < batches and not totals_only:
            attend(step, score)
            score = next_score
        if step >= 2:
            sums = add_gradient(step - 2, sums)
    if totals_only:
        out_ref[0], out_ref[1] = sums
        return

    starts = [[first, second], [first - inner_rate * sums[0], second - inner_rate * sums[1]]]
    if across:
        for way, other in enumerate((before_ref, after_ref)):
            for i in range(2):
                starts[way][i] = starts[way][i] - inner_rate * other[i]
    gates = gate_ref[:, :dim]

    def enter_models(b):
        (w0, v0), (w1, v1) = starts
        w0, v0 = (w0 - inner_rate * sum_first_ref[b], v0 - inner_rate * sum_second_ref[b])
        if b > 0:
            w1, v1 = (w1 + inner_rate * sum_first_ref[b - 1], v1 + inner_rate * sum_second_ref[b - 1])
        pairs = [jnp.concatenate(split(w), axis=0) for w in (w0, w1)]
        z = dot(queries(b), jnp.concatenate(pairs, axis=1), NN)
        return split(gelu(z)), [split(centred(v)) for v in (v0, v1)]

    def leave_models(entered):
        (high, low), seconds = entered
        total = 0.0
        for way in range(2):
            cols = slice(way * inner, (way + 1) * inner)
            u = project((high[:, cols], low[:, cols]), seconds[way])
            total = total + gates[way : way + 1] * (u * norm_scale(u))
        return total

    entered = enter_models(0)
    for b in range(batches):
        next_entered = None if b + 1 == batches else enter_models(b + 1)
        q = queries(b)[:, :dim].astype(f32)
        result = leave_models(entered)
        result = encode(attended_ref[here(b), :] + (gates[0:1] + gates[1:2]) * q + result)
        out_ref[b] = jnp.concatenate([result[: part // 2], result[part // 2 :]], axis=1)
        entered = next_entered


def work_on_head(x, w_first, w_second, gate_pairs, others=(), totals_only=False):
    dim, inner = w_first.shape[1:]
    tokens = x.shape[0] * (x.shape[1] * 2 // 3)
    if totals_only:
        out = pltpu.VMEM((2, dim, inner), f32)
    else:
        out = pltpu.VMEM((GROUP, tokens // GROUP // 2, LANES), bf16)
    return pl.pallas_call(
        functools.partial(head_kernel, totals_only=totals_only, across=len(others) > 0),
        in_specs=[in_vmem] + [in_hbm] * 3 + [in_vmem] * len(others),
        out_specs=in_vmem,
        scratch_shapes=[
            pltpu.VMEM((dim, inner), f32),
            pltpu.VMEM((dim, inner), f32),
            pltpu.VMEM(gate_pairs.shape, f32),
            pltpu.SemaphoreType.DMA((3,)),
            pltpu.VMEM((tokens, LANES), bf16),
            pltpu.VMEM((tokens, LANES), bf16),
            pltpu.VMEM((tokens, inner), bf16),
            pltpu.VMEM((tokens, inner), bf16),
            pltpu.VMEM((tokens, inner), f32),
            pltpu.VMEM((tokens, 3 * dim), bf16),
            pltpu.VMEM((tokens, dim), f32),
            pltpu.VMEM((GROUP, dim, inner), f32),
            pltpu.VMEM((GROUP, dim, inner), f32),
        ],
        out_shape=out,
        compiler_params=pltpu.CompilerParams(vmem_limit_bytes=52 * 2**20),
        name="totals" if totals_only else "head",
    )(vmem(x), hbm(w_first), hbm(w_second), hbm(gate_pairs), *[vmem(other) for other in others])


def unpack_kernel(packed_ref, out_hbm, rows_ref, copied):
    half = packed_ref.shape[1]
    left = left_half(half)
    copies = []
    for second in range(2):
        here = pl.ds(second * half, half)
        for pair in range(rows_ref.shape[1] // LANES):
            even = packed_ref[2 * pair]
            odd = packed_ref[2 * pair + 1]
            cols = slice(pair * LANES, (pair + 1) * LANES)
            if second:
                rows_ref[here, cols] = decode(jnp.where(left, half_turn(even), odd))
            else:
                rows_ref[here, cols] = decode(jnp.where(left, even, half_turn(odd)))
        copies.append(pltpu.make_async_copy(rows_ref.at[here], out_hbm.at[here], copied.at[second]))
        copies[second].start()
    for copy in copies:
        copy.wait()


def unpack(packed, heads_here):
    out = (2 * packed.shape[1], heads_here * HEAD_DIM)
    return pl.pallas_call(
        unpack_kernel,
        in_specs=[in_vmem],
        out_specs=in_hbm,
        out_shape=jax.ShapeDtypeStruct(out, f32),
        scratch_shapes=[pltpu.VMEM(out, f32), pltpu.SemaphoreType.DMA((2,))],
        name="unpack",
    )(vmem(packed))


def on_device(queries, key_rows, value_rows, w_first, w_second, gate_pairs):
    seg, sides = (lax.axis_size("seg"), lax.axis_size("head"))
    heads_here = w_first.shape[0]
    segments = seg // GROUP
    assert heads_here <= GROUP
    both = [[s * GROUP * sides + i for i in range(GROUP * sides)] for s in range(segments)]
    lines = [[s * GROUP + i for i in range(GROUP)] for s in range(segments)]
    w_second = jnp.swapaxes(w_second, 1, 2)
    x = pack(queries, key_rows, value_rows, heads_here, sides)
    x = lax.all_to_all(x, ("seg", "head"), 0, 0, tiled=True, axis_index_groups=both)
    others = ()
    if segments > 1:
        totals = work_on_head(x, w_first, w_second, gate_pairs, totals_only=True)
        across = [[s * GROUP + i for s in range(segments)] for i in range(GROUP)]
        here = lax.axis_index("seg") // GROUP
        totals = lax.all_gather(totals, "seg", axis_index_groups=across)
        order = jnp.arange(segments).reshape(-1, 1, 1, 1)
        before = jnp.sum(jnp.where(order < here, totals, 0.0), axis=0)
        after = jnp.sum(jnp.where(order > here, totals, 0.0), axis=0)
        others = (before, after)
    out = work_on_head(x, w_first, w_second, gate_pairs, others)
    out = lax.all_to_all(out, "seg", 0, 0, tiled=True, axis_index_groups=lines)
    return unpack(out, heads_here)


def solution(mesh):
    in_specs = (
        P(("seg", "head"), None),
        P(("seg", "head"), None),
        P(("seg", "head"), None),
        P("head", None, None),
        P("head", None, None),
        P(None, "head"),
    )
    return jax.shard_map(
        on_device, mesh=mesh, in_specs=in_specs, out_specs=P("seg", "head"), check_vma=False
    )
```
